256 devices in a mesh: tm: 8 (over x_lo, y), rows: 32 (over z, x_hi, core).
Axes of the slice: x: 4 (x_hi: 2, x_lo: 2; x = x_hi * 2 + x_lo), y: 4, z: 8, core: 2. Of those that a mesh axis runs over, the one named last changes fastest.
Arguments:
- video_in: bfloat16 [16, 32, 192, 128], P('tm', 'rows'), may hold values from -6 to 6
- kernels: bfloat16 [2, 5184, 192], replicated, may hold values from -0.15625 to 0.15625
- cotangent: bfloat16 [16, 32, 192, 128], P('tm', 'rows'), may hold values from -6 to 6
Outputs:
- input_grad: bfloat16 [16, 32, 192, 128], P('tm', 'rows')
- kernel_grad: float32 [2, 5184, 192], P(None, 'rows')
The draws below stay inside these ranges and needn't reach their ends.
All inputs are finite; a program needn't handle non-finite values.
Results may differ from the reference program's by a relative error of at most 0.01.
Values may be sent and summed in bfloat16 or wider, within the bound.
A program may use at most 128 MiB of HBM per device.

```python
import math
import jax
import jax.numpy as jnp

C = 192
LAYERS = 2
COLS = 128
FRAMES = 16
ROWS = 32
TAPS = 5184


def level_of(rng, extent, cuts, smallest, largest):
    loudness, own = 1.0, jax.random.fold_in(rng, 6)
    for dim, blocks in cuts:
        draws = jnp.exp(jax.random.uniform(jax.random.fold_in(own, dim), (blocks,), jnp.float32, smallest / len(cuts), largest / len(cuts)))
        loudness = loudness * jnp.repeat(draws, extent[dim] // blocks).reshape([-1 if axis == dim else 1 for axis in range(len(extent))])
    return loudness


def scatter_about(rng, shape, width, most, split=(), kind=jnp.bfloat16):
    loudness = level_of(rng, shape, split, -0.22, 0.18) if split else 1.0
    entries = jax.random.normal(rng, shape, jnp.float32) * width * loudness
    return jnp.minimum(jnp.maximum(entries, -most), most).astype(kind)


def setup_inputs(seed: int = 0) -> dict:
    streams_of = jax.random.split(jax.random.key(seed), 4)
    return {
        "video_in": scatter_about(streams_of[0], (FRAMES, ROWS, C, COLS), 1.0, 6.0, ((0, 8), (1, 32))),
        "kernels": scatter_about(streams_of[1], (LAYERS, TAPS, C), (9 * C) ** -0.5, 0.15625),
        "cotangent": scatter_about(streams_of[2], (FRAMES, ROWS, C, COLS), 1.0, 6.0, ((0, 8), (1, 32))),
    }


def conv_forward(acts, kernel):
    frame_count, row_count, channel, col_count = acts.shape
    padded = jnp.pad(acts.astype(jnp.float32), ((2, 0), (1, 1), (0, 0), (1, 1)))
    result = jnp.zeros((frame_count, row_count, channel, col_count), jnp.float32)
    for time_tap in range(3):
        for row_tap in range(3):
            for col_tap in range(3):
                weight_tap = kernel[time_tap * 9 + row_tap * 3 + col_tap].astype(jnp.float32)
                window = padded[time_tap:time_tap + frame_count, row_tap:row_tap + row_count, :, col_tap:col_tap + col_count]
                result = result + jnp.einsum('frcw,cd->frdw', window, weight_tap)
    return result

def conv_backward(grad, kernel):
    frame_count, row_count, channel, col_count = grad.shape
    padded = jnp.pad(grad.astype(jnp.float32), ((0, 2), (1, 1), (0, 0), (1, 1)))
    result = jnp.zeros((frame_count, row_count, channel, col_count), jnp.float32)
    for time_tap in range(3):
        for row_tap in range(3):
            for col_tap in range(3):
                weight_tap = kernel[time_tap * 9 + row_tap * 3 + col_tap].astype(jnp.float32)
                window = padded[2 - time_tap:2 - time_tap + frame_count, 2 - row_tap:2 - row_tap + row_count, :, 2 - col_tap:2 - col_tap + col_count]
                result = result + jnp.einsum('frdw,cd->frcw', window, weight_tap)
    return result

def kernel_terms(acts, grad):
    frame_count, row_count, channel, col_count = acts.shape
    padded = jnp.pad(acts.astype(jnp.float32), ((2, 0), (1, 1), (0, 0), (1, 1)))
    grad_wide = grad.astype(jnp.float32)
    pieces = []
    for time_tap in range(3):
        for row_tap in range(3):
            for col_tap in range(3):
                window = padded[time_tap:time_tap + frame_count, row_tap:row_tap + row_count, :, col_tap:col_tap + col_count]
                pieces.append(jnp.einsum('frcw,frdw->cd', window, grad_wide))
    return jnp.concatenate(pieces, axis=0)

def reference(video_in, kernels, cotangent):
    inputs = []
    acts_list = []
    state = video_in
    for layer_id in range(LAYERS):
        acts = jax.nn.silu(state.astype(jnp.float32)).astype(jnp.bfloat16)
        inputs.append(state)
        acts_list.append(acts)
        state = conv_forward(acts, kernels[layer_id].reshape(27, C, C)).astype(jnp.bfloat16)
    grad = cotangent
    terms = [None] * LAYERS
    for layer_id in reversed(range(LAYERS)):
        kernel = kernels[layer_id].reshape(27, C, C)
        terms[layer_id] = kernel_terms(acts_list[layer_id], grad)
        back = conv_backward(grad, kernel)
        wide_in = inputs[layer_id].astype(jnp.float32)
        sigma = jax.nn.sigmoid(wide_in)
        grad = (back * sigma * (1.0 + wide_in * (1.0 - sigma))).astype(jnp.bfloat16)
    scale_factor = 1.0 / math.sqrt(FRAMES * ROWS * COLS)
    return (grad, jnp.stack(terms) * scale_factor)
```

```python
import math

import jax
import jax.numpy as jnp
from jax import lax
from jax.experimental import pallas as pl
from jax.experimental.pallas import tpu as pltpu
from jax.sharding import PartitionSpec as P

MESH = pl.DeviceIdType.MESH
F32 = jnp.float32
BF16 = jnp.bfloat16
C = 192
W = 128
TM = 8
ROWS = 32
HALF = 2592
CHUNK = 176


def dot(a, b):
    return lax.dot_general(a, b, (((1,), (0,)), ((), ())), preferred_element_type=F32)


def dot_nt(a, b):
    return lax.dot_general(a, b, (((1,), (1,)), ((), ())), preferred_element_type=F32)


def lane_shift(value, by):
    rolled = pltpu.roll(value, by % W, 1)
    col = lax.broadcasted_iota(jnp.int32, value.shape, 1)
    edge = 0 if by == 1 else W - 1
    return jnp.where(col == edge, 0.0, rolled)


def sublane_shift(value, by):
    rolled = pltpu.roll(value, by % W, 0)
    row = lax.broadcasted_iota(jnp.int32, value.shape, 0)
    edge = 0 if by == 1 else W - 1
    return jnp.where(row == edge, 0.0, rolled)


def silu_parts(value):
    sigma = jax.nn.sigmoid(value)
    return value * sigma, sigma * (1.0 + value * (1.0 - sigma))


def group_a(y):
    return 16 * jnp.minimum(3 * y, 8)


def group_b(y):
    return 16 * (y + jnp.where(y >= 2, 1, 0))


def chunk_start(j):
    return pl.multiple_of(16 * ((81 * j) // 8), 16)


def kernel(
    video, kernels, cotangent, in_grad, k_grad,
    k1, k2, vext, cext, gext, acts, acts_t, acc_t, acc, x1, wa, wb, pair_in, summed,
    r1a, r1b, ta, tb, r2a, r2b, ub, r3, r4, final,
    load_sem, halo_send, halo_recv, pair_send, pair_recv,
    s1_send, s1_recv, s2_send, s2_recv, s3_send, s3_recv, s4_send, s4_recv,
):
    t = lax.axis_index("tm")
    r = lax.axis_index("rows")
    xl, y = t // 4, t % 4
    z, xh, c = r // 4, (r // 2) % 2, r % 2
    x = 2 * xh + xl
    has_up, has_down = r > 0, r < ROWS - 1
    has_past, has_future = t > 0, t < TM - 1

    loads = [
        pltpu.make_async_copy(video, vext.at[1, 1], load_sem.at[0]),
        pltpu.make_async_copy(cotangent, cext.at[0, 1], load_sem.at[1]),
        pltpu.make_async_copy(kernels.at[0], k1, load_sem.at[2]),
        pltpu.make_async_copy(kernels.at[1], k2, load_sem.at[3]),
    ]
    for load in loads:
        load.start()

    barrier = pltpu.get_barrier_semaphore()

    def greet(device):
        pl.semaphore_signal(barrier, inc=1, device_id=device, device_id_type=MESH)

    @pl.when(has_up)
    def _():
        greet((t, r - 1))

    @pl.when(has_down)
    def _():
        greet((t, r + 1))

    for e in range(1, 8):
        greet((lax.rem(t + e, 8), r))
        greet((t, lax.rem(z + e, 8) * 4 + xh * 2 + c))
    greet((xl * 4 + y, z * 4 + (1 - xh) * 2 + c))
    greet(((1 - xl) * 4 + y, z * 4 + (1 - xh) * 2 + c))

    neighbours = jnp.where(has_up, 1, 0) + jnp.where(has_down, 1, 0)
    pl.semaphore_wait(barrier, 16 + neighbours)

    exts = (vext, cext, gext)

    def own_of(field):
        return 1 if field == 0 else 0

    def side_of(field):
        return 0 if field == 0 else 1

    def halo_copy(field, part, where, src):
        if where == 1:
            device = (t + 1, r) if field == 0 else (t - 1, r)
            slot = (side_of(field), 1)
        else:
            device = (t, r - 1) if where == 0 else (t, r + 1)
            slot = (part, 2 - where)
        return pltpu.make_async_remote_copy(
            src_ref=src,
            dst_ref=exts[field].at[slot],
            send_sem=halo_send.at[field, part, where],
            recv_sem=halo_recv.at[field, slot[0], slot[1]],
            device_id=device,
            device_id_type=MESH,
        )

    def sends_time(field):
        return has_future if field == 0 else has_past

    def gets_time(field):
        return has_past if field == 0 else has_future

    row_side = {0: has_up, 2: has_down}

    def start_own(field, src):
        @pl.when(sends_time(field))
        def _():
            halo_copy(field, own_of(field), 1, src).start()

        for where in (0, 2):
            @pl.when(row_side[where])
            def _(where=where):
                halo_copy(field, own_of(field), where, src).start()

    def wait_slot(field, part, row):
        pltpu.make_async_remote_copy(
            src_ref=exts[field].at[part, row],
            dst_ref=exts[field].at[part, row],
            send_sem=halo_send.at[field, part, row],
            recv_sem=halo_recv.at[field, part, row],
            device_id=(t, r),
            device_id_type=MESH,
        ).wait_recv()

    def forward(field):
        side = side_of(field)

        @pl.when(gets_time(field))
        def _():
            wait_slot(field, side, 1)

        for where in (0, 2):
            @pl.when(jnp.logical_and(gets_time(field), row_side[where]))
            def _(where=where):
                halo_copy(field, side, where, exts[field].at[side, 1]).start()

    def wait_rows(field, part):
        for row in (0, 2):
            cond = row_side[row]
            if part == side_of(field):
                cond = jnp.logical_and(cond, gets_time(field))

            @pl.when(cond)
            def _(row=row):
                wait_slot(field, part, row)

    def finish_sends(field, src):
        side = side_of(field)

        @pl.when(sends_time(field))
        def _():
            halo_copy(field, own_of(field), 1, src).wait_send()

        for where in (0, 2):
            @pl.when(row_side[where])
            def _(where=where):
                halo_copy(field, own_of(field), where, src).wait_send()

            @pl.when(jnp.logical_and(gets_time(field), row_side[where]))
            def _(where=where):
                halo_copy(field, side, where, exts[field].at[side, 1]).wait_send()

    start_own(0, video)
    start_own(1, cotangent)

    zeros_block = jnp.zeros((2, C, W), BF16)
    for field in range(3):
        side = side_of(field)
        for row in range(3):
            cond = jnp.logical_not(gets_time(field))
            if row != 1:
                cond = jnp.logical_or(cond, jnp.logical_not(row_side[row]))

            @pl.when(cond)
            def _(field=field, side=side, row=row):
                exts[field][side, row] = zeros_block

            if row != 1:
                @pl.when(jnp.logical_not(row_side[row]))
                def _(field=field, row=row):
                    exts[field][own_of(field), row] = zeros_block

    def activate(part, row):
        for f in range(2):
            at = 2 * part + f
            value, _ = silu_parts(vext[part, row, f].astype(F32))
            acts[at, row] = value.astype(BF16)
            acts_t[row, at * W : (at + 1) * W, :] = jnp.transpose(value).astype(BF16)

    loads[0].wait()
    activate(1, 1)
    forward(0)
    forward(1)
    activate(0, 1)
    loads[2].wait()

    def conv_taps(row, tt, first):
        lhs = acts_t[row, tt * W : (tt + 2) * W, :]
        for q in range(3):
            tap = tt * 9 + row * 3 + q
            term = dot(lhs, k1[tap * C : (tap + 1) * C, :])
            if first:
                acc_t[q] = term
            else:
                acc_t[q] += term

    for tt in range(3):
        conv_taps(1, tt, tt == 0)
    wait_rows(0, 1)
    activate(1, 0)
    activate(1, 2)
    conv_taps(0, 2, False)
    conv_taps(2, 2, False)
    wait_rows(0, 0)
    activate(0, 0)
    activate(0, 2)
    for row in (0, 2):
        for tt in range(2):
            conv_taps(row, tt, False)
    for f in range(2):
        rows = slice(f * W, (f + 1) * W)
        out = sublane_shift(acc_t[0, rows], 1) + acc_t[1, rows] + sublane_shift(acc_t[2, rows], -1)
        x1[f] = jnp.transpose(out).astype(BF16)

    def field_pair(ext, tt, p):
        at = (2 - tt, 3 - tt)
        return jnp.concatenate([ext[a // 2, 2 - p, a % 2] for a in at], axis=1)

    def back_taps(ext, k_ref, tt, p, first):
        g = tt * 3 + p
        term = dot(k_ref[g * 576 : (g + 1) * 576, :], field_pair(ext, tt, p))
        if first:
            acc[...] = term
        else:
            acc[...] += term

    def back_sum(f):
        cols = slice(f * W, (f + 1) * W)
        return (
            lane_shift(acc[0:C, cols], -1)
            + acc[C : 2 * C, cols]
            + lane_shift(acc[2 * C : 3 * C, cols], 1)
        )

    loads[1].wait()
    loads[3].wait()
    wait_rows(1, 0)
    wait_rows(1, 1)
    for p in range(3):
        for tt in range(3):
            back_taps(cext, k2, tt, p, p == 0 and tt == 0)
    for f in range(2):
        _, slope = silu_parts(x1[f].astype(F32))
        gext[0, 1, f] = (back_sum(f) * slope).astype(BF16)
    start_own(2, gext.at[0, 1])

    zeros64 = jnp.zeros((64, 2 * W), BF16)

    def store_term(layer, start, term):
        n = term.shape[0]
        wa[layer, start : start + n, :] = term[:, :W].astype(BF16)
        if start < HALF:
            wb[layer, start : start + n, :] = term[:, W:].astype(BF16)
        else:
            wb[layer, start - HALF : start - HALF + n, :] += term[:, W:].astype(BF16)

    def widened(value, upper):
        lo, hi = value[:W], value[W:C]
        return jnp.concatenate([lo, zeros64, hi] if upper else [lo, hi, zeros64], axis=0)

    pair_blocks = []
    for h in range(2):
        for bx in range(2):
            for b in range(6):
                zi, kind = b // 3, b % 3
                z_to = 2 * h + zi + (4 if kind == 2 else 0)
                pair_blocks.append((h, bx, b, kind == 1, 4 * z_to + 2 * bx))

    def block_src(layer, packed, j):
        ref = wb if packed else wa
        return ref.at[layer, pl.ds(chunk_start(j), CHUNK), :]

    sibling = (t, r + 1 - 2 * c)

    def pair_copy(layer, h, bx, b, packed, j0):
        return pltpu.make_async_remote_copy(
            src_ref=block_src(layer, packed, j0 + 1 - c),
            dst_ref=pair_in.at[layer, h, bx, b],
            send_sem=pair_send.at[layer, h, bx, b],
            recv_sem=pair_recv.at[layer, h, bx, b],
            device_id=sibling,
            device_id_type=MESH,
        )

    def pair_start(layer):
        for block in pair_blocks:
            pair_copy(layer, *block).start()

    a2 = []
    for f in range(2):
        value, _ = silu_parts(x1[f].astype(F32))
        a2.append([lane_shift(value, 1), value, lane_shift(value, -1)])
    a2_taps = jnp.concatenate(
        [jnp.concatenate([a2[f][q].astype(BF16) for f in range(2)], axis=1) for q in range(3)], axis=0
    )
    acts2 = a2_taps
    for g in range(9):
        pair = field_pair(cext, g // 3, g % 3)
        if g < 4:
            store_term(1, 576 * g, dot_nt(acts2, widened(pair, False)))
        elif g == 4:
            store_term(1, 576 * g, dot_nt(acts2[:288], widened(pair, False)))
            store_term(1, HALF, dot_nt(acts2[288:], widened(pair, True)))
        else:
            store_term(1, 576 * g, dot_nt(acts2, widened(pair, True)))
    pair_start(1)

    g1 = [gext[0, 1, f].astype(F32) for f in range(2)]
    g1_taps = []
    for q in range(3):
        by = {0: -1, 2: 1}.get(q)
        cols = [g1[f] if by is None else lane_shift(g1[f], by) for f in range(2)]
        g1_taps.append(jnp.concatenate([v.astype(BF16) for v in cols], axis=1))
    g1_low = [widened(v, False) for v in g1_taps]
    g1_high = [widened(v, True) for v in g1_taps]
    for g in range(9):
        tt, p = g // 3, g % 3
        lhs = jnp.concatenate([acts[tt, p], acts[tt + 1, p]], axis=1)
        for q in range(3):
            start = 576 * g + C * q
            if start + C <= HALF:
                store_term(0, start, dot_nt(lhs, g1_low[q]))
            elif start >= HALF:
                store_term(0, start, dot_nt(lhs, g1_high[q]))
            else:
                store_term(0, start, dot_nt(lhs[:96], g1_low[q]))
                store_term(0, HALF, dot_nt(lhs[96:], g1_high[q]))
    pair_start(0)

    def dev(nxl, ny, nz, nxh):
        return (nxl * 4 + ny, nz * 4 + nxh * 2 + c)

    def s1_copies(layer):
        out = []
        for d in range(1, 4):
            ny = lax.rem(y + d, 4)
            out.append(
                pltpu.make_async_remote_copy(
                    src_ref=summed.at[layer, 0, :, :, pl.ds(pl.multiple_of(group_a(ny), 16), 48), :],
                    dst_ref=r1a.at[layer, d - 1],
                    send_sem=s1_send.at[layer, 0, d - 1],
                    recv_sem=s1_recv.at[layer, 0, d - 1],
                    device_id=dev(xl, ny, z, xh),
                    device_id_type=MESH,
                )
            )
            nx = lax.rem(x + d, 4)
            out.append(
                pltpu.make_async_remote_copy(
                    src_ref=summed.at[layer, 1, nx // 2, :, pl.ds(pl.multiple_of(80 * (nx % 2), 16), 96), :],
                    dst_ref=r1b.at[layer, d - 1],
                    send_sem=s1_send.at[layer, 1, d - 1],
                    recv_sem=s1_recv.at[layer, 1, d - 1],
                    device_id=dev(nx % 2, y, z, nx // 2),
                    device_id_type=MESH,
                )
            )
        return out

    def s2_copies(layer):
        out = []
        for d in range(1, 4):
            nx = lax.rem(x + d, 4)
            out.append(
                pltpu.make_async_remote_copy(
                    src_ref=ta.at[layer, nx // 2, :, pl.ds(pl.multiple_of(16 * (nx % 2), 16), 32), :],
                    dst_ref=r2a.at[layer, d - 1],
                    send_sem=s2_send.at[layer, 0, d - 1],
                    recv_sem=s2_recv.at[layer, 0, d - 1],
                    device_id=dev(nx % 2, y, z, nx // 2),
                    device_id_type=MESH,
                )
            )
            ny = lax.rem(y + d, 4)
            out.append(
                pltpu.make_async_remote_copy(
                    src_ref=tb.at[layer, :, pl.ds(pl.multiple_of(group_b(ny), 16), 32), :],
                    dst_ref=r2b.at[layer, d - 1],
                    send_sem=s2_send.at[layer, 1, d - 1],
                    recv_sem=s2_recv.at[layer, 1, d - 1],
                    device_id=dev(xl, ny, z, xh),
                    device_id_type=MESH,
                )
            )
        return out

    def z_block(nz):
        return (nz % 4) // 2, 3 * (nz % 2) + nz // 4

    def s3_copies(layer):
        out = []
        for d in range(1, 8):
            nz = lax.rem(z + d, 8)
            nh, nb = z_block(nz)
            out.append(
                pltpu.make_async_remote_copy(
                    src_ref=ub.at[layer, nh, pl.ds(nb, 2)],
                    dst_ref=r3.at[layer, d - 1],
                    send_sem=s3_send.at[layer, d - 1],
                    recv_sem=s3_recv.at[layer, d - 1],
                    device_id=dev(xl, y, nz, xh),
                    device_id_type=MESH,
                )
            )
        return out

    def s4_copies(layer):
        out = []
        for e in range(1, 8):
            out.append(
                pltpu.make_async_remote_copy(
                    src_ref=r4.at[layer, 0],
                    dst_ref=r4.at[layer, e],
                    send_sem=s4_send.at[layer, e - 1],
                    recv_sem=s4_recv.at[layer, e - 1],
                    device_id=(lax.rem(t + e, 8), r),
                    device_id_type=MESH,
                )
            )
        return out

    def wide(value):
        return value.astype(F32)

    def stage1(layer):
        for h, bx, b, packed, j0 in pair_blocks:
            pair_copy(layer, h, bx, b, packed, j0).wait()
            own = block_src(layer, packed, j0 + c)[...]
            summed[layer, h, bx, b] = (wide(own) + wide(pair_in[layer, h, bx, b])).astype(BF16)
        for copy in s1_copies(layer):
            copy.start()

    def stage2(layer):
        for copy in s1_copies(layer):
            copy.wait()
        for bx in range(2):
            for b in range(6):
                own = summed[layer, 0, bx, b, pl.ds(pl.multiple_of(group_a(y), 16), 48), :]
                ta[layer, bx, b] = (
                    wide(own) + wide(r1a[layer, 0, bx, b]) + wide(r1a[layer, 1, bx, b]) + wide(r1a[layer, 2, bx, b])
                ).astype(BF16)
        for b in range(6):
            own = summed[layer, 1, xh, b, pl.ds(pl.multiple_of(80 * xl, 16), 96), :]
            tb[layer, b] = (
                wide(own) + wide(r1b[layer, 0, b]) + wide(r1b[layer, 1, b]) + wide(r1b[layer, 2, b])
            ).astype(BF16)
        for copy in s2_copies(layer):
            copy.start()

    def stage3(layer):
        for copy in s2_copies(layer):
            copy.wait()
        for b in range(6):
            own = ta[layer, xh, b, pl.ds(pl.multiple_of(16 * xl, 16), 32), :]
            ub[layer, 0, b] = (
                wide(own) + wide(r2a[layer, 0, b]) + wide(r2a[layer, 1, b]) + wide(r2a[layer, 2, b])
            ).astype(BF16)
            own = tb[layer, b, pl.ds(pl.multiple_of(group_b(y), 16), 32), :]
            ub[layer, 1, b] = (
                wide(own) + wide(r2b[layer, 0, b]) + wide(r2b[layer, 1, b]) + wide(r2b[layer, 2, b])
            ).astype(BF16)
        for copy in s3_copies(layer):
            copy.start()

    my_half, my_block = z_block(z)
    scale = 1.0 / math.sqrt(TM * 2 * ROWS * W)

    def stage4(layer):
        for copy in s3_copies(layer):
            copy.wait()
        for k in range(2):
            total = wide(ub[layer, my_half, my_block + k])
            for d in range(7):
                total += wide(r3[layer, d, k])
            r4[layer, 0, k] = total.astype(BF16)
        for copy in s4_copies(layer):
            copy.start()

    def stage5(layer):
        for copy in s4_copies(layer):
            copy.wait()
        upper = z // 4
        for e in range(8):
            u = lax.rem(t + 8 - e, 8)
            uy, ux = u % 4, u // 4
            at_a = jnp.minimum(3 * uy, 8) + ux
            at_b = 5 * ux + uy + jnp.where(uy >= 2, 1, 0)
            start = pl.multiple_of(16 * jnp.where(my_half == 0, at_a, at_b), 16)
            main = wide(r4[layer, e, upper]) * scale
            rest = wide(r4[layer, e, 1 - upper]) * scale
            rest = jnp.where(upper == 0, rest, pltpu.roll(rest, 64, 1))
            final[pl.ds(start, 32), :W] = main
            final[pl.ds(start, 32), W:] = rest
        off = 4 * (z % 2) + 2 * xh + c
        for k in range(8):
            @pl.when(off == k)
            def _(k=k):
                k_grad[layer] = final[2 * k : 2 * k + 162, :C]

    stage1(1)
    forward(2)
    stage1(0)

    def back_rows(p):
        for tt in range(3):
            back_taps(gext, k1, tt, p, p == 1 and tt == 0)

    back_rows(1)
    wait_rows(2, 0)
    wait_rows(2, 1)
    back_rows(0)
    back_rows(2)
    for f in range(2):
        _, slope = silu_parts(vext[1, 1, f].astype(F32))
        in_grad[f, 0] = (back_sum(f) * slope).astype(BF16)

    stage2(1)
    stage2(0)
    stage3(1)
    stage3(0)
    stage4(1)
    stage4(0)
    stage5(1)
    stage5(0)

    finish_sends(0, video)
    finish_sends(1, cotangent)
    finish_sends(2, gext.at[0, 1])


def on_device(video_in, kernels, cotangent):
    dma = pltpu.SemaphoreType.DMA
    any_spec = pl.BlockSpec(memory_space=pl.ANY)
    vmem_spec = pl.BlockSpec(memory_space=pltpu.VMEM)
    return pl.pallas_call(
        kernel,
        out_shape=(
            jax.ShapeDtypeStruct((2, 1, C, W), BF16),
            jax.ShapeDtypeStruct((2, 162, C), F32),
        ),
        in_specs=[any_spec] * 3,
        out_specs=(vmem_spec, vmem_spec),
        scratch_shapes=[
            pltpu.VMEM((5184, C), BF16),
            pltpu.VMEM((5184, C), BF16),
            pltpu.VMEM((2, 3, 2, C, W), BF16),
            pltpu.VMEM((2, 3, 2, C, W), BF16),
            pltpu.VMEM((2, 3, 2, C, W), BF16),
            pltpu.VMEM((4, 3, C, W), BF16),
            pltpu.VMEM((3, 4 * W, C), BF16),
            pltpu.VMEM((3, 2 * W, C), F32),
            pltpu.VMEM((3 * C, 2 * W), F32),
            pltpu.VMEM((2, C, W), BF16),
            pltpu.VMEM((2, 5184, W), BF16),
            pltpu.VMEM((2, HALF, W), BF16),
            pltpu.VMEM((2, 2, 2, 6, CHUNK, W), BF16),
            pltpu.VMEM((2, 2, 2, 6, CHUNK, W), BF16),
            pltpu.VMEM((2, 3, 2, 6, 48, W), BF16),
            pltpu.VMEM((2, 3, 6, 96, W), BF16),
            pltpu.VMEM((2, 2, 6, 48, W), BF16),
            pltpu.VMEM((2, 6, 96, W), BF16),
            pltpu.VMEM((2, 3, 6, 32, W), BF16),
            pltpu.VMEM((2, 3, 6, 32, W), BF16),
            pltpu.VMEM((2, 2, 6, 32, W), BF16),
            pltpu.VMEM((2, 7, 2, 32, W), BF16),
            pltpu.VMEM((2, 8, 2, 32, W), BF16),
            pltpu.VMEM((CHUNK, 2 * W), F32),
            dma((4,)),
            dma((3, 2, 3)),
            dma((3, 2, 3)),
            dma((2, 2, 2, 6)),
            dma((2, 2, 2, 6)),
            dma((2, 2, 3)),
            dma((2, 2, 3)),
            dma((2, 2, 3)),
            dma((2, 2, 3)),
            dma((2, 7)),
            dma((2, 7)),
            dma((2, 7)),
            dma((2, 7)),
        ],
        compiler_params=pltpu.CompilerParams(
            collective_id=0, has_side_effects=True, vmem_limit_bytes=56 * 2**20
        ),
        cost_estimate=pl.CostEstimate(flops=2600000000, bytes_accessed=6000000, transcendentals=500000),
    )(video_in.reshape(2, C, W), kernels, cotangent.reshape(2, C, W))


def solution(mesh):
    return jax.shard_map(
        on_device,
        mesh=mesh,
        in_specs=(P("tm", "rows", None, None), P(), P("tm", "rows", None, None)),
        out_specs=(P("tm", "rows", None, None), P(None, "rows", None)),
        check_vma=False,
    )
```

```python
import math

import jax
import jax.numpy as jnp
from jax import lax
from jax.experimental import pallas as pl
from jax.experimental.pallas import tpu as pltpu
from jax.sharding import PartitionSpec as P

MESH = pl.DeviceIdType.MESH
F32 = jnp.float32
BF16 = jnp.bfloat16
C = 192
W = 128
TM = 8
ROWS = 32
HALF = 2592
CHUNK = 176


def dot(a, b):
    return lax.dot_general(a, b, (((1,), (0,)), ((), ())), preferred_element_type=F32)


def dot_nt(a, b):
    return lax.dot_general(a, b, (((1,), (1,)), ((), ())), preferred_element_type=F32)


def lane_shift(value, by):
    rolled = pltpu.roll(value, by % W, 1)
    col = lax.broadcasted_iota(jnp.int32, value.shape, 1)
    edge = 0 if by == 1 else W - 1
    return jnp.where(col == edge, 0.0, rolled)


def silu_parts(value):
    sigma = jax.nn.sigmoid(value)
    return value * sigma, sigma * (1.0 + value * (1.0 - sigma))


def group_a(y):
    return 16 * jnp.minimum(3 * y, 8)


def group_b(y):
    return 16 * (y + jnp.where(y >= 2, 1, 0))


def chunk_start(j):
    return pl.multiple_of(16 * ((81 * j) // 8), 16)


def kernel(
    video, kernels, cotangent, in_grad, k_grad,
    k1t, k2t, k1, k2, vext, cext, gext, stack, acts2, acc, x1, wa, wb, pair_in, summed,
    r1a, r1b, ta, tb, r2a, r2b, ub, r3, r4, final,
    load_sem, halo_send, halo_recv, pair_send, pair_recv,
    s1_send, s1_recv, s2_send, s2_recv, s3_send, s3_recv, s4_send, s4_recv,
):
    t = lax.axis_index("tm")
    r = lax.axis_index("rows")
    xl, y = t // 4, t % 4
    z, xh, c = r // 4, (r // 2) % 2, r % 2
    x = 2 * xh + xl
    has_up, has_down = r > 0, r < ROWS - 1
    has_past, has_future = t > 0, t < TM - 1

    loads = [
        pltpu.make_async_copy(video, vext.at[1, 1], load_sem.at[0]),
        pltpu.make_async_copy(cotangent, cext.at[0, 1], load_sem.at[1]),
        pltpu.make_async_copy(kernels.at[0], k1t, load_sem.at[2]),
        pltpu.make_async_copy(kernels.at[1], k2t, load_sem.at[3]),
    ]
    for load in loads:
        load.start()

    barrier = pltpu.get_barrier_semaphore()

    def greet(device):
        pl.semaphore_signal(barrier, inc=1, device_id=device, device_id_type=MESH)

    @pl.when(has_up)
    def _():
        greet((t, r - 1))

    @pl.when(has_down)
    def _():
        greet((t, r + 1))

    for e in range(1, 8):
        greet((lax.rem(t + e, 8), r))
        greet((t, lax.rem(z + e, 8) * 4 + xh * 2 + c))
    greet((xl * 4 + y, z * 4 + (1 - xh) * 2 + c))
    greet(((1 - xl) * 4 + y, z * 4 + (1 - xh) * 2 + c))

    neighbours = jnp.where(has_up, 1, 0) + jnp.where(has_down, 1, 0)
    pl.semaphore_wait(barrier, 16 + neighbours)

    exts = (vext, cext, gext)

    def own_of(field):
        return 1 if field == 0 else 0

    def side_of(field):
        return 0 if field == 0 else 1

    def halo_copy(field, part, where, src):
        if where == 1:
            device = (t + 1, r) if field == 0 else (t - 1, r)
            slot = (side_of(field), 1)
        else:
            device = (t, r - 1) if where == 0 else (t, r + 1)
            slot = (part, 2 - where)
        return pltpu.make_async_remote_copy(
            src_ref=src,
            dst_ref=exts[field].at[slot],
            send_sem=halo_send.at[field, part, where],
            recv_sem=halo_recv.at[field, slot[0], slot[1]],
            device_id=device,
            device_id_type=MESH,
        )

    def sends_time(field):
        return has_future if field == 0 else has_past

    def gets_time(field):
        return has_past if field == 0 else has_future

    row_side = {0: has_up, 2: has_down}

    def start_own(field, src):
        @pl.when(sends_time(field))
        def _():
            halo_copy(field, own_of(field), 1, src).start()

        for where in (0, 2):
            @pl.when(row_side[where])
            def _(where=where):
                halo_copy(field, own_of(field), where, src).start()

    def wait_slot(field, part, row):
        pltpu.make_async_remote_copy(
            src_ref=exts[field].at[part, row],
            dst_ref=exts[field].at[part, row],
            send_sem=halo_send.at[field, part, row],
            recv_sem=halo_recv.at[field, part, row],
            device_id=(t, r),
            device_id_type=MESH,
        ).wait_recv()

    def forward(field):
        side = side_of(field)

        @pl.when(gets_time(field))
        def _():
            wait_slot(field, side, 1)

        for where in (0, 2):
            @pl.when(jnp.logical_and(gets_time(field), row_side[where]))
            def _(where=where):
                halo_copy(field, side, where, exts[field].at[side, 1]).start()

    def wait_rows(field, part):
        for row in (0, 2):
            cond = row_side[row]
            if part == side_of(field):
                cond = jnp.logical_and(cond, gets_time(field))

            @pl.when(cond)
            def _(row=row):
                wait_slot(field, part, row)

    def finish_sends(field, src):
        side = side_of(field)

        @pl.when(sends_time(field))
        def _():
            halo_copy(field, own_of(field), 1, src).wait_send()

        for where in (0, 2):
            @pl.when(row_side[where])
            def _(where=where):
                halo_copy(field, own_of(field), where, src).wait_send()

            @pl.when(jnp.logical_and(gets_time(field), row_side[where]))
            def _(where=where):
                halo_copy(field, side, where, exts[field].at[side, 1]).wait_send()

    start_own(0, video)
    start_own(1, cotangent)

    zeros_block = jnp.zeros((2, C, W), BF16)
    for field in range(3):
        side = side_of(field)
        for row in range(3):
            cond = jnp.logical_not(gets_time(field))
            if row != 1:
                cond = jnp.logical_or(cond, jnp.logical_not(row_side[row]))

            @pl.when(cond)
            def _(field=field, side=side, row=row):
                exts[field][side, row] = zeros_block

            if row != 1:
                @pl.when(jnp.logical_not(row_side[row]))
                def _(field=field, row=row):
                    exts[field][own_of(field), row] = zeros_block

    def activate(part, row):
        for f in range(2):
            at = 2 * part + f
            value, _ = silu_parts(vext[part, row, f].astype(F32))
            shifted = (lane_shift(value, 1), value, lane_shift(value, -1))
            for q in range(3):
                block = shifted[q].astype(BF16)
                for to in range(2):
                    tt = at - to
                    if 0 <= tt <= 2:
                        start = (tt * 9 + row * 3 + q) * C
                        stack[start : start + C, to * W : (to + 1) * W] = block

    def turn(src, dst):
        for start in range(0, 5184, W):
            n = min(W, 5184 - start)
            dst[start : start + n, :] = jnp.transpose(src[:, start : start + n])

    loads[0].wait()
    activate(1, 1)
    loads[3].wait()
    forward(0)
    turn(k2t, k2)
    forward(1)
    activate(0, 1)
    wait_rows(0, 1)
    activate(1, 0)
    activate(1, 2)
    loads[2].wait()
    late = dot(k1t[:, 3456:], stack[3456:, :])
    wait_rows(0, 0)
    activate(0, 0)
    activate(0, 2)
    out = late + dot(k1t[:, :3456], stack[:3456, :])
    for f in range(2):
        x1[f] = out[:, f * W : (f + 1) * W].astype(BF16)

    zeros64 = jnp.zeros((64, 2 * W), BF16)

    def widened(value, upper):
        lo, hi = value[:W], value[W:C]
        return jnp.concatenate([lo, zeros64, hi] if upper else [lo, hi, zeros64], axis=0)

    def field_pair(ext, tt, p):
        at = (2 - tt, 3 - tt)
        return jnp.concatenate([ext[a // 2, 2 - p, a % 2] for a in at], axis=1)

    pair_blocks = []
    for h in range(2):
        for bx in range(2):
            for b in range(6):
                zi, kind = b // 3, b % 3
                z_to = 2 * h + zi + (4 if kind == 2 else 0)
                pair_blocks.append((h, bx, b, kind == 1, 4 * z_to + 2 * bx))

    def ready_at(block):
        j = block[4] % 16 + 1
        return -(-(16 * ((81 * j) // 8) + CHUNK) // 288) - 1

    def block_src(layer, packed, j):
        ref = wb if packed else wa
        return ref.at[layer, pl.ds(chunk_start(j), CHUNK), :]

    sibling = (t, r + 1 - 2 * c)

    def pair_copy(layer, h, bx, b, packed, j0):
        return pltpu.make_async_remote_copy(
            src_ref=block_src(layer, packed, j0 + 1 - c),
            dst_ref=pair_in.at[layer, h, bx, b],
            send_sem=pair_send.at[layer, h, bx, b],
            recv_sem=pair_recv.at[layer, h, bx, b],
            device_id=sibling,
            device_id_type=MESH,
        )

    def kernel_terms(layer, term):
        for k in range(9):
            at = 288 * k
            low, high = term(k, False), term(k + 9, True)
            wa[layer, at : at + 288, :] = low[:, :W].astype(BF16)
            wa[layer, HALF + at : HALF + at + 288, :] = high[:, :W].astype(BF16)
            wb[layer, at : at + 288, :] = (low[:, W:] + high[:, W:]).astype(BF16)
            for block in pair_blocks:
                if ready_at(block) == k:
                    pair_copy(layer, *block).start()

    def back_terms(ext, k_ref, p, first):
        for tt in range(3):
            g = tt * 3 + p
            term = dot(k_ref[g * 576 : (g + 1) * 576, :], field_pair(ext, tt, p))
            if first and tt == 0:
                acc[...] = term
            else:
                acc[...] += term

    def back_sum(f):
        cols = slice(f * W, (f + 1) * W)
        return (
            lane_shift(acc[0:C, cols], -1)
            + acc[C : 2 * C, cols]
            + lane_shift(acc[2 * C : 3 * C, cols], 1)
        )

    for f in range(2):
        value, _ = silu_parts(x1[f].astype(F32))
        shifted = (lane_shift(value, 1), value, lane_shift(value, -1))
        for q in range(3):
            acts2[q * C : (q + 1) * C, f * W : (f + 1) * W] = shifted[q].astype(BF16)
    loads[1].wait()
    wait_rows(1, 0)
    wait_rows(1, 1)

    def second_term(hg, upper):
        g, part = hg // 2, hg % 2
        pair = widened(field_pair(cext, g // 3, g % 3), upper)
        return dot_nt(acts2[288 * part : 288 * part + 288, :], pair)

    kernel_terms(1, second_term)

    for p in range(3):
        back_terms(cext, k2, p, p == 0)
    for f in range(2):
        _, slope = silu_parts(x1[f].astype(F32))
        gext[0, 1, f] = (back_sum(f) * slope).astype(BF16)
    start_own(2, gext.at[0, 1])

    def first_term(hg, upper):
        pair = jnp.concatenate([gext[0, 1, 0], gext[0, 1, 1]], axis=1)
        return dot_nt(stack[288 * hg : 288 * hg + 288, :], widened(pair, upper))

    def dev(nxl, ny, nz, nxh):
        return (nxl * 4 + ny, nz * 4 + nxh * 2 + c)

    def s1_copies(layer):
        out = []
        for d in range(1, 4):
            ny = lax.rem(y + d, 4)
            out.append(
                pltpu.make_async_remote_copy(
                    src_ref=summed.at[layer, 0, :, :, pl.ds(pl.multiple_of(group_a(ny), 16), 48), :],
                    dst_ref=r1a.at[layer, d - 1],
                    send_sem=s1_send.at[layer, 0, d - 1],
                    recv_sem=s1_recv.at[layer, 0, d - 1],
                    device_id=dev(xl, ny, z, xh),
                    device_id_type=MESH,
                )
            )
            nx = lax.rem(x + d, 4)
            out.append(
                pltpu.make_async_remote_copy(
                    src_ref=summed.at[layer, 1, nx // 2, :, pl.ds(pl.multiple_of(80 * (nx % 2), 16), 96), :],
                    dst_ref=r1b.at[layer, d - 1],
                    send_sem=s1_send.at[layer, 1, d - 1],
                    recv_sem=s1_recv.at[layer, 1, d - 1],
                    device_id=dev(nx % 2, y, z, nx // 2),
                    device_id_type=MESH,
                )
            )
        return out

    def s2_copies(layer):
        out = []
        for d in range(1, 4):
            nx = lax.rem(x + d, 4)
            out.append(
                pltpu.make_async_remote_copy(
                    src_ref=ta.at[layer, nx // 2, :, pl.ds(pl.multiple_of(16 * (nx % 2), 16), 32), :],
                    dst_ref=r2a.at[layer, d - 1],
                    send_sem=s2_send.at[layer, 0, d - 1],
                    recv_sem=s2_recv.at[layer, 0, d - 1],
                    device_id=dev(nx % 2, y, z, nx // 2),
                    device_id_type=MESH,
                )
            )
            ny = lax.rem(y + d, 4)
            out.append(
                pltpu.make_async_remote_copy(
                    src_ref=tb.at[layer, :, pl.ds(pl.multiple_of(group_b(ny), 16), 32), :],
                    dst_ref=r2b.at[layer, d - 1],
                    send_sem=s2_send.at[layer, 1, d - 1],
                    recv_sem=s2_recv.at[layer, 1, d - 1],
                    device_id=dev(xl, ny, z, xh),
                    device_id_type=MESH,
                )
            )
        return out

    def z_block(nz):
        return (nz % 4) // 2, 3 * (nz % 2) + nz // 4

    def s3_copies(layer):
        out = []
        for d in range(1, 8):
            nz = lax.rem(z + d, 8)
            nh, nb = z_block(nz)
            out.append(
                pltpu.make_async_remote_copy(
                    src_ref=ub.at[layer, nh, pl.ds(nb, 2)],
                    dst_ref=r3.at[layer, d - 1],
                    send_sem=s3_send.at[layer, d - 1],
                    recv_sem=s3_recv.at[layer, d - 1],
                    device_id=dev(xl, y, nz, xh),
                    device_id_type=MESH,
                )
            )
        return out

    def s4_copies(layer):
        out = []
        for e in range(1, 8):
            out.append(
                pltpu.make_async_remote_copy(
                    src_ref=r4.at[layer, 0],
                    dst_ref=r4.at[layer, e],
                    send_sem=s4_send.at[layer, e - 1],
                    recv_sem=s4_recv.at[layer, e - 1],
                    device_id=(lax.rem(t + e, 8), r),
                    device_id_type=MESH,
                )
            )
        return out

    def wide(value):
        return value.astype(F32)

    def stage1(layer):
        for h, bx, b, packed, j0 in pair_blocks:
            pair_copy(layer, h, bx, b, packed, j0).wait()
            own = block_src(layer, packed, j0 + c)[...]
            summed[layer, h, bx, b] = (wide(own) + wide(pair_in[layer, h, bx, b])).astype(BF16)
        for copy in s1_copies(layer):
            copy.start()

    def stage2(layer):
        for copy in s1_copies(layer):
            copy.wait()
        for bx in range(2):
            for b in range(6):
                own = summed[layer, 0, bx, b, pl.ds(pl.multiple_of(group_a(y), 16), 48), :]
                ta[layer, bx, b] = (
                    wide(own) + wide(r1a[layer, 0, bx, b]) + wide(r1a[layer, 1, bx, b]) + wide(r1a[layer, 2, bx, b])
                ).astype(BF16)
        for b in range(6):
            own = summed[layer, 1, xh, b, pl.ds(pl.multiple_of(80 * xl, 16), 96), :]
            tb[layer, b] = (
                wide(own) + wide(r1b[layer, 0, b]) + wide(r1b[layer, 1, b]) + wide(r1b[layer, 2, b])
            ).astype(BF16)
        for copy in s2_copies(layer):
            copy.start()

    def stage3(layer):
        for copy in s2_copies(layer):
            copy.wait()
        for b in range(6):
            own = ta[layer, xh, b, pl.ds(pl.multiple_of(16 * xl, 16), 32), :]
            ub[layer, 0, b] = (
                wide(own) + wide(r2a[layer, 0, b]) + wide(r2a[layer, 1, b]) + wide(r2a[layer, 2, b])
            ).astype(BF16)
            own = tb[layer, b, pl.ds(pl.multiple_of(group_b(y), 16), 32), :]
            ub[layer, 1, b] = (
                wide(own) + wide(r2b[layer, 0, b]) + wide(r2b[layer, 1, b]) + wide(r2b[layer, 2, b])
            ).astype(BF16)
        for copy in s3_copies(layer):
            copy.start()

    my_half, my_block = z_block(z)
    scale = 1.0 / math.sqrt(TM * 2 * ROWS * W)

    def stage4(layer):
        for copy in s3_copies(layer):
            copy.wait()
        for k in range(2):
            total = wide(ub[layer, my_half, my_block + k])
            for d in range(7):
                total += wide(r3[layer, d, k])
            r4[layer, 0, k] = total.astype(BF16)
        for copy in s4_copies(layer):
            copy.start()

    def stage5(layer):
        for copy in s4_copies(layer):
            copy.wait()
        upper = z // 4
        for e in range(8):
            u = lax.rem(t + 8 - e, 8)
            uy, ux = u % 4, u // 4
            at_a = jnp.minimum(3 * uy, 8) + ux
            at_b = 5 * ux + uy + jnp.where(uy >= 2, 1, 0)
            start = pl.multiple_of(16 * jnp.where(my_half == 0, at_a, at_b), 16)
            main = wide(r4[layer, e, upper]) * scale
            rest = wide(r4[layer, e, 1 - upper]) * scale
            rest = jnp.where(upper == 0, rest, pltpu.roll(rest, 64, 1))
            final[pl.ds(start, 32), :W] = main
            final[pl.ds(start, 32), W:] = rest
        off = 4 * (z % 2) + 2 * xh + c
        for k in range(8):
            @pl.when(off == k)
            def _(k=k):
                k_grad[layer] = final[2 * k : 2 * k + 162, :C]

    stage1(1)
    kernel_terms(0, first_term)
    forward(2)
    stage1(0)
    turn(k1t, k1)
    back_terms(gext, k1, 1, True)
    wait_rows(2, 0)
    wait_rows(2, 1)
    back_terms(gext, k1, 0, False)
    back_terms(gext, k1, 2, False)
    for f in range(2):
        _, slope = silu_parts(vext[1, 1, f].astype(F32))
        in_grad[f, 0] = (back_sum(f) * slope).astype(BF16)

    stage2(1)
    stage2(0)
    stage3(1)
    stage3(0)
    stage4(1)
    stage4(0)
    stage5(1)
    stage5(0)

    finish_sends(0, video)
    finish_sends(1, cotangent)
    finish_sends(2, gext.at[0, 1])


def on_device(video_in, kernels, cotangent):
    dma = pltpu.SemaphoreType.DMA
    any_spec = pl.BlockSpec(memory_space=pl.ANY)
    vmem_spec = pl.BlockSpec(memory_space=pltpu.VMEM)
    return pl.pallas_call(
        kernel,
        out_shape=(
            jax.ShapeDtypeStruct((2, 1, C, W), BF16),
            jax.ShapeDtypeStruct((2, 162, C), F32),
        ),
        in_specs=[any_spec] * 3,
        out_specs=(vmem_spec, vmem_spec),
        scratch_shapes=[
            pltpu.VMEM((C, 5184), BF16),
            pltpu.VMEM((C, 5184), BF16),
            pltpu.VMEM((5184, C), BF16),
            pltpu.VMEM((5184, C), BF16),
            pltpu.VMEM((2, 3, 2, C, W), BF16),
            pltpu.VMEM((2, 3, 2, C, W), BF16),
            pltpu.VMEM((2, 3, 2, C, W), BF16),
            pltpu.VMEM((5184, 2 * W), BF16),
            pltpu.VMEM((3 * C, 2 * W), BF16),
            pltpu.VMEM((3 * C, 2 * W), F32),
            pltpu.VMEM((2, C, W), BF16),
            pltpu.VMEM((2, 5184, W), BF16),
            pltpu.VMEM((2, HALF, W), BF16),
            pltpu.VMEM((2, 2, 2, 6, CHUNK, W), BF16),
            pltpu.VMEM((2, 2, 2, 6, CHUNK, W), BF16),
            pltpu.VMEM((2, 3, 2, 6, 48, W), BF16),
            pltpu.VMEM((2, 3, 6, 96, W), BF16),
            pltpu.VMEM((2, 2, 6, 48, W), BF16),
            pltpu.VMEM((2, 6, 96, W), BF16),
            pltpu.VMEM((2, 3, 6, 32, W), BF16),
            pltpu.VMEM((2, 3, 6, 32, W), BF16),
            pltpu.VMEM((2, 2, 6, 32, W), BF16),
            pltpu.VMEM((2, 7, 2, 32, W), BF16),
            pltpu.VMEM((2, 8, 2, 32, W), BF16),
            pltpu.VMEM((CHUNK, 2 * W), F32),
            dma((4,)),
            dma((3, 2, 3)),
            dma((3, 2, 3)),
            dma((2, 2, 2, 6)),
            dma((2, 2, 2, 6)),
            dma((2, 2, 3)),
            dma((2, 2, 3)),
            dma((2, 2, 3)),
            dma((2, 2, 3)),
            dma((2, 7)),
            dma((2, 7)),
            dma((2, 7)),
            dma((2, 7)),
        ],
        compiler_params=pltpu.CompilerParams(
            collective_id=0, has_side_effects=True, vmem_limit_bytes=56 * 2**20
        ),
        cost_estimate=pl.CostEstimate(flops=2600000000, bytes_accessed=6000000, transcendentals=500000),
    )(video_in.reshape(2, C, W), jnp.swapaxes(kernels, 1, 2), cotangent.reshape(2, C, W))


def solution(mesh):
    return jax.shard_map(
        on_device,
        mesh=mesh,
        in_specs=(P("tm", "rows", None, None), P(), P("tm", "rows", None, None)),
        out_specs=(P("tm", "rows", None, None), P(None, "rows", None)),
        check_vma=False,
    )
```

```python
import math

import jax
import jax.numpy as jnp
from jax import lax
from jax.experimental import pallas as pl
from jax.experimental.pallas import tpu as pltpu
from jax.sharding import PartitionSpec as P

MESH = pl.DeviceIdType.MESH
F32 = jnp.float32
BF16 = jnp.bfloat16
C = 192
W = 128
TM = 8
ROWS = 32
HALF = 2592
CHUNK = 176


def dot(a, b):
    return lax.dot_general(a, b, (((1,), (0,)), ((), ())), preferred_element_type=F32)


def dot_nt(a, b):
    return lax.dot_general(a, b, (((1,), (1,)), ((), ())), preferred_element_type=F32)


def lane_shift(value, by):
    rolled = pltpu.roll(value, by % W, 1)
    col = lax.broadcasted_iota(jnp.int32, value.shape, 1)
    edge = 0 if by == 1 else W - 1
    return jnp.where(col == edge, 0.0, rolled)


def silu_parts(value):
    sigma = jax.nn.sigmoid(value)
    return value * sigma, sigma * (1.0 + value * (1.0 - sigma))


def chunk_start(j):
    return pl.multiple_of(16 * ((81 * j) // 8), 16)


def kernel(
    video, kernels, cotangent, in_grad, k_grad,
    k1t, k2t, k1, k2, vext, cext, gext, stack, acts2, acc, x1, wa, wb, pair_in, summed,
    r1a, r1b, ta, tb, r2a, r2b, ub, r3, rz1, tz, rz2, tc, rp, r4, final,
    load_sem, halo_send, halo_recv, pair_send, pair_recv,
    s1_send, s1_recv, s2_send, s2_recv, s3_send, s3_recv, z1_send, z1_recv, z2_send, z2_recv,
    p_send, p_recv, s4_send, s4_recv,
):
    t = lax.axis_index("tm")
    r = lax.axis_index("rows")
    xl, y = t // 4, t % 4
    z, xh, c = r // 4, (r // 2) % 2, r % 2
    x = 2 * xh + xl
    has_far = jnp.logical_and(r > 0, r < ROWS - 1)
    far_row, sibling_row = r - 1 + 2 * c, r + 1 - 2 * c
    far_slot, sibling_slot = 2 * c, 2 - 2 * c
    has_past, has_future = t > 0, t < TM - 1

    loads = [
        pltpu.make_async_copy(video, vext.at[1, 1], load_sem.at[0]),
        pltpu.make_async_copy(cotangent, cext.at[0, 1], load_sem.at[1]),
        pltpu.make_async_copy(kernels.at[0], k1t, load_sem.at[2]),
        pltpu.make_async_copy(kernels.at[1], k2t, load_sem.at[3]),
    ]
    for load in loads:
        load.start()

    barrier = pltpu.get_barrier_semaphore()

    def greet(device):
        pl.semaphore_signal(barrier, inc=1, device_id=device, device_id_type=MESH)

    for e in range(1, 8):
        greet((lax.rem(t + e, 8), r))
        greet((t, lax.rem(z + e, 8) * 4 + xh * 2 + c))
    for e in range(8):
        greet((lax.rem(t + e, 8), z * 4 + (1 - xh) * 2 + c))
    greet((t, sibling_row))

    @pl.when(has_far)
    def _():
        greet((t, far_row))

    pl.semaphore_wait(barrier, 23 + jnp.where(has_far, 1, 0))

    exts = (vext, cext, gext)

    def own_of(field):
        return 1 if field == 0 else 0

    def side_of(field):
        return 0 if field == 0 else 1

    def sends_time(field):
        return has_future if field == 0 else has_past

    def gets_time(field):
        return has_past if field == 0 else has_future

    def halo_copy(field, which, src=None):
        own, side, ext = own_of(field), side_of(field), exts[field]
        time_device = (t + 1, r) if field == 0 else (t - 1, r)
        if which == 0:
            device, part, row = (t, far_row), own, 2 - 2 * c
        elif which == 1:
            device, part, row = (t, sibling_row), own, 2 * c
        elif which == 2:
            device, part, row = time_device, side, 1
        elif which == 3:
            src, device, part, row = ext.at[own, far_slot], time_device, side, far_slot
        else:
            src, device, part, row = ext.at[side, 1], (t, sibling_row), side, 2 * c
        return pltpu.make_async_remote_copy(
            src_ref=src,
            dst_ref=ext.at[part, row],
            send_sem=halo_send.at[field, which],
            recv_sem=halo_recv.at[field, part, row],
            device_id=device,
            device_id_type=MESH,
        )

    def sends(field, which):
        return (
            has_far,
            None,
            sends_time(field),
            jnp.logical_and(has_far, sends_time(field)),
            gets_time(field),
        )[which]

    def when(cond, act):
        if cond is None:
            act()
        else:
            pl.when(cond)(act)

    def start_own(field, src):
        for which in (0, 2, 1):
            when(sends(field, which), lambda which=which: halo_copy(field, which, src).start())

    def wait_slot(field, part, row):
        pltpu.make_async_remote_copy(
            src_ref=exts[field].at[part, row],
            dst_ref=exts[field].at[part, row],
            send_sem=halo_send.at[field, 0],
            recv_sem=halo_recv.at[field, part, row],
            device_id=(t, sibling_row),
            device_id_type=MESH,
        ).wait_recv()

    def forward(field):
        own, side = own_of(field), side_of(field)
        when(has_far, lambda: wait_slot(field, own, far_slot))
        when(sends(field, 3), lambda: halo_copy(field, 3).start())
        when(gets_time(field), lambda: wait_slot(field, side, 1))
        when(sends(field, 4), lambda: halo_copy(field, 4).start())

    def wait_corners(field):
        side = side_of(field)
        when(jnp.logical_and(has_far, gets_time(field)), lambda: wait_slot(field, side, far_slot))
        when(gets_time(field), lambda: wait_slot(field, side, sibling_slot))

    def finish_sends(field, src):
        for which in range(5):
            when(sends(field, which), lambda which=which: halo_copy(field, which, src).wait_send())

    start_own(0, video)
    start_own(1, cotangent)

    zeros_block = jnp.zeros((2, C, W), BF16)

    def clear(field, part, row):
        exts[field][part, row] = zeros_block

    for field in range(3):
        own, side = own_of(field), side_of(field)
        no_time = jnp.logical_not(gets_time(field))
        no_far = jnp.logical_not(has_far)
        when(no_far, lambda: clear(field, own, far_slot))
        when(no_time, lambda: clear(field, side, 1))
        when(no_time, lambda: clear(field, side, sibling_slot))
        when(jnp.logical_or(no_time, no_far), lambda: clear(field, side, far_slot))

    def activate(part, row):
        for f in range(2):
            at = 2 * part + f
            value, _ = silu_parts(vext[part, row, f].astype(F32))
            shifted = (lane_shift(value, 1), value, lane_shift(value, -1))
            for q in range(3):
                block = shifted[q].astype(BF16)
                for to in range(2):
                    tt = at - to
                    if 0 <= tt <= 2:
                        start = (tt * 9 + row * 3 + q) * C
                        stack[start : start + C, to * W : (to + 1) * W] = block

    def turn(src, dst):
        for start in range(0, 5184, W):
            n = min(W, 5184 - start)
            dst[start : start + n, :] = jnp.transpose(src[:, start : start + n])

    loads[0].wait()
    activate(1, 1)
    loads[3].wait()
    turn(k2t, k2)
    loads[2].wait()
    turn(k1t, k1)
    forward(0)
    activate(0, 1)
    wait_slot(0, 1, sibling_slot)
    activate(1, 0)
    activate(1, 2)
    forward(1)
    late = dot(k1t[:, 3456:], stack[3456:, :])
    wait_corners(0)
    activate(0, 0)
    activate(0, 2)
    out = late + dot(k1t[:, :3456], stack[:3456, :])
    for f in range(2):
        x1[f] = out[:, f * W : (f + 1) * W].astype(BF16)

    zeros64 = jnp.zeros((64, 2 * W), BF16)

    def widened(value, upper):
        lo, hi = value[:W], value[W:C]
        return jnp.concatenate([lo, zeros64, hi] if upper else [lo, hi, zeros64], axis=0)

    def field_pair(ext, tt, p):
        at = (2 - tt, 3 - tt)
        return jnp.concatenate([ext[a // 2, 2 - p, a % 2] for a in at], axis=1)

    pair_blocks = []
    for h in range(2):
        for bx in range(2):
            for b in range(6):
                zi, kind = b // 3, b % 3
                z_to = 2 * h + zi + (4 if kind == 2 else 0)
                pair_blocks.append((h, bx, b, kind == 1, 4 * z_to + 2 * bx))

    def ready_at(block):
        j = block[4] % 16 + 1
        return -(-(16 * ((81 * j) // 8) + CHUNK) // 288) - 1

    def block_src(layer, packed, j):
        ref = wb if packed else wa
        return ref.at[layer, pl.ds(chunk_start(j), CHUNK), :]

    sibling = (t, sibling_row)

    def pair_copy(layer, h, bx, b, packed, j0):
        return pltpu.make_async_remote_copy(
            src_ref=block_src(layer, packed, j0 + 1 - c),
            dst_ref=pair_in.at[layer, h, bx, b],
            send_sem=pair_send.at[layer, h, bx, b],
            recv_sem=pair_recv.at[layer, h, bx, b],
            device_id=sibling,
            device_id_type=MESH,
        )

    def kernel_terms(layer, term):
        for k in range(9):
            at = 288 * k
            low, high = term(k, False), term(k + 9, True)
            wa[layer, at : at + 288, :] = low[:, :W].astype(BF16)
            wa[layer, HALF + at : HALF + at + 288, :] = high[:, :W].astype(BF16)
            wb[layer, at : at + 288, :] = (low[:, W:] + high[:, W:]).astype(BF16)
            for block in pair_blocks:
                if ready_at(block) == k:
                    pair_copy(layer, *block).start()

    def back_terms(ext, k_ref, p, first):
        for tt in range(3):
            g = tt * 3 + p
            term = dot(k_ref[g * 576 : (g + 1) * 576, :], field_pair(ext, tt, p))
            if first and tt == 0:
                acc[...] = term
            else:
                acc[...] += term

    def back_sum(f):
        cols = slice(f * W, (f + 1) * W)
        return (
            lane_shift(acc[0:C, cols], -1)
            + acc[C : 2 * C, cols]
            + lane_shift(acc[2 * C : 3 * C, cols], 1)
        )

    for f in range(2):
        value, _ = silu_parts(x1[f].astype(F32))
        shifted = (lane_shift(value, 1), value, lane_shift(value, -1))
        for q in range(3):
            acts2[q * C : (q + 1) * C, f * W : (f + 1) * W] = shifted[q].astype(BF16)
    loads[1].wait()
    wait_slot(1, 0, sibling_slot)
    wait_corners(1)

    def second_term(hg, upper):
        g, part = hg // 2, hg % 2
        pair = widened(field_pair(cext, g // 3, g % 3), upper)
        return dot_nt(acts2[288 * part : 288 * part + 288, :], pair)

    kernel_terms(1, second_term)

    for p in range(3):
        back_terms(cext, k2, p, p == 0)
    for f in range(2):
        _, slope = silu_parts(x1[f].astype(F32))
        gext[0, 1, f] = (back_sum(f) * slope).astype(BF16)
    start_own(2, gext.at[0, 1])

    def first_term(hg, upper):
        pair = jnp.concatenate([gext[0, 1, 0], gext[0, 1, 1]], axis=1)
        return dot_nt(stack[288 * hg : 288 * hg + 288, :], widened(pair, upper))

    def dev(nxl, ny, nz, nxh):
        return (nxl * 4 + ny, nz * 4 + nxh * 2 + c)

    def remote(src, dst, sems, at, device):
        return pltpu.make_async_remote_copy(
            src_ref=src,
            dst_ref=dst,
            send_sem=sems[0].at[at],
            recv_sem=sems[1].at[at],
            device_id=device,
            device_id_type=MESH,
        )

    def rows_at(start, n):
        return pl.ds(pl.multiple_of(start, 16), n)

    def z_block(nz):
        return (nz % 4) // 2, 3 * (nz % 2) + nz // 4

    def s1_copies(layer):
        out = []
        for d in range(1, 4):
            ny, nx = lax.rem(y + d, 4), lax.rem(x + d, 4)
            src = summed.at[layer, 0, :, :, rows_at(32 * ny, 32), :]
            out.append(remote(src, r1a.at[layer, d - 1], (s1_send, s1_recv), (layer, 0, d - 1), dev(xl, ny, z, xh)))
            src = summed.at[layer, 1, nx // 2, :, rows_at(64 * (nx % 2), 64), :]
            out.append(
                remote(src, r1b.at[layer, d - 1], (s1_send, s1_recv), (layer, 1, d - 1), dev(nx % 2, y, z, nx // 2))
            )
        return out

    def s2_copies(layer):
        out = []
        for d in range(1, 4):
            ny, nx = lax.rem(y + d, 4), lax.rem(x + d, 4)
            src = ta.at[layer, nx // 2, :, rows_at(16 * (nx % 2), 16), :]
            out.append(
                remote(src, r2a.at[layer, d - 1], (s2_send, s2_recv), (layer, 0, d - 1), dev(nx % 2, y, z, nx // 2))
            )
            src = tb.at[layer, :, rows_at(16 * ny, 16), :]
            out.append(remote(src, r2b.at[layer, d - 1], (s2_send, s2_recv), (layer, 1, d - 1), dev(xl, ny, z, xh)))
        return out

    def s3_copies(layer):
        out = []
        for d in range(1, 8):
            nz = lax.rem(z + d, 8)
            nh, nb = z_block(nz)
            src = ub.at[layer, nh, pl.ds(nb, 2)]
            out.append(remote(src, r3.at[layer, d - 1], (s3_send, s3_recv), (layer, d - 1), dev(xl, y, nz, xh)))
        return out

    def z_off(steps):
        return lax.rem(z + steps * (1 - 2 * c) + 8, 8)

    def z_part(layer, nz):
        nh, nb = z_block(nz)
        return summed.at[layer, nh, :, pl.ds(nb, 2), 128:CHUNK, :]

    relays = ((4, 1), (2, 1), (-3, -1))

    def z1_copies(layer):
        out = []
        for k, (to, hop) in enumerate(relays):
            src = z_part(layer, z_off(to))
            out.append(remote(src, rz1.at[layer, k], (z1_send, z1_recv), (layer, k), dev(xl, y, z_off(hop), xh)))
        return out

    def z2_copies(layer):
        out = []
        for k, (to, hop) in enumerate(relays):
            device = dev(xl, y, z_off(to - hop), xh)
            out.append(remote(tz.at[layer, k], rz2.at[layer, k], (z2_send, z2_recv), (layer, k), device))
        src = z_part(layer, z_off(-1))
        out.append(remote(src, rz2.at[layer, 3], (z2_send, z2_recv), (layer, 3), dev(xl, y, z_off(-1), xh)))
        return out

    upper = z // 4
    place = 4 * x + y

    def plane_src(layer, nx, ny):
        return tc.at[layer, nx // 2, lax.rem(upper + nx, 2), rows_at(16 * jnp.minimum(ny, 2), 16), :]

    def plane_copies(layer):
        out = []
        for e in range(1, 16):
            to = lax.rem(place + e, 16)
            nx, ny = to // 4, to % 4
            src = plane_src(layer, nx, ny)
            device = dev(nx % 2, ny, z, nx // 2)
            out.append(remote(src, rp.at[layer, e - 1], (p_send, p_recv), (layer, e - 1), device))
        return out

    def s4_copies(layer):
        out = []
        for e in range(1, 8):
            device = (lax.rem(t + e, 8), r)
            out.append(remote(r4.at[layer, 0], r4.at[layer, e], (s4_send, s4_recv), (layer, e - 1), device))
        return out

    def wide(value):
        return value.astype(F32)

    def start_all(copies):
        for copy in copies:
            copy.start()

    def wait_all(copies):
        for copy in copies:
            copy.wait()

    def stage1(layer):
        for h, bx, b, packed, j0 in pair_blocks:
            pair_copy(layer, h, bx, b, packed, j0).wait()
            own = block_src(layer, packed, j0 + c)[...]
            summed[layer, h, bx, b] = (wide(own) + wide(pair_in[layer, h, bx, b])).astype(BF16)
        start_all(z1_copies(layer))
        start_all(s1_copies(layer))

    def relay(layer):
        wait_all(z1_copies(layer))
        for k, (to, hop) in enumerate(relays):
            own = z_part(layer, z_off(to - hop))[...]
            tz[layer, k] = (wide(own) + wide(rz1[layer, k])).astype(BF16)
        start_all(z2_copies(layer))

    def plane(layer):
        wait_all(z2_copies(layer))
        total = wide(z_part(layer, z)[...])
        for k in range(4):
            total += wide(rz2[layer, k])
        tc[layer] = total.astype(BF16)
        start_all(plane_copies(layer))

    def stage2(layer):
        wait_all(s1_copies(layer))
        own = summed[layer, 0, :, :, rows_at(32 * y, 32), :]
        ta[layer] = (wide(own) + wide(r1a[layer, 0]) + wide(r1a[layer, 1]) + wide(r1a[layer, 2])).astype(BF16)
        own = summed[layer, 1, xh, :, rows_at(64 * xl, 64), :]
        tb[layer] = (wide(own) + wide(r1b[layer, 0]) + wide(r1b[layer, 1]) + wide(r1b[layer, 2])).astype(BF16)
        start_all(s2_copies(layer))

    def stage3(layer):
        wait_all(s2_copies(layer))
        own = ta[layer, xh, :, rows_at(16 * xl, 16), :]
        ub[layer, 0] = (wide(own) + wide(r2a[layer, 0]) + wide(r2a[layer, 1]) + wide(r2a[layer, 2])).astype(BF16)
        own = tb[layer, :, rows_at(16 * y, 16), :]
        ub[layer, 1] = (wide(own) + wide(r2b[layer, 0]) + wide(r2b[layer, 1]) + wide(r2b[layer, 2])).astype(BF16)
        start_all(s3_copies(layer))

    my_half, my_block = z_block(z)
    scale = 1.0 / math.sqrt(TM * 2 * ROWS * W)

    def stage4(layer):
        wait_all(plane_copies(layer))
        total = wide(plane_src(layer, x, y)[...])
        for e in range(15):
            total += wide(rp[layer, e])
        r4[layer, 0, 2] = total.astype(BF16)
        wait_all(s3_copies(layer))
        for k in range(2):
            total = wide(ub[layer, my_half, my_block + k])
            for d in range(7):
                total += wide(r3[layer, d, k])
            r4[layer, 0, k] = total.astype(BF16)
        start_all(s4_copies(layer))

    def unpacked(value):
        return jnp.where(upper == 0, value, pltpu.roll(value, 64, 1))

    def stage5(layer):
        wait_all(s4_copies(layer))
        for e in range(8):
            u = lax.rem(t + 8 - e, 8)
            uy, ux = u % 4, u // 4
            start = jnp.where(my_half == 0, 32 * uy + 16 * ux, 64 * ux + 16 * uy)
            final[rows_at(start, 16), :W] = wide(r4[layer, e, upper]) * scale
            final[rows_at(start, 16), W:] = unpacked(wide(r4[layer, e, 1 - upper]) * scale)
            start = 128 + 16 * jnp.minimum(uy, 2)
            value = wide(r4[layer, e, 2]) * scale

            @pl.when(jnp.logical_and(ux == 0, uy < 3))
            def _(start=start, value=value):
                final[rows_at(start, 16), :W] = value

            @pl.when(jnp.logical_and(ux == 1, uy < 3))
            def _(start=start, value=value):
                final[rows_at(start, 16), W:] = unpacked(value)

        off = 4 * (z % 2) + 2 * xh + c
        for k in range(8):
            @pl.when(off == k)
            def _(k=k):
                k_grad[layer] = final[2 * k : 2 * k + 162, :C]

    stage1(1)
    kernel_terms(0, first_term)
    forward(2)
    relay(1)
    stage1(0)
    stage2(1)
    plane(1)
    wait_slot(2, 0, sibling_slot)
    back_terms(gext, k1, 1, True)
    relay(0)
    stage3(1)
    wait_corners(2)
    back_terms(gext, k1, 0, False)
    back_terms(gext, k1, 2, False)
    for f in range(2):
        _, slope = silu_parts(vext[1, 1, f].astype(F32))
        in_grad[f, 0] = (back_sum(f) * slope).astype(BF16)

    stage2(0)
    plane(0)
    stage4(1)
    stage3(0)
    stage4(0)
    stage5(1)
    stage5(0)

    finish_sends(0, video)
    finish_sends(1, cotangent)
    finish_sends(2, gext.at[0, 1])


def on_device(video_in, kernels, cotangent):
    dma = pltpu.SemaphoreType.DMA
    any_spec = pl.BlockSpec(memory_space=pl.ANY)
    vmem_spec = pl.BlockSpec(memory_space=pltpu.VMEM)
    return pl.pallas_call(
        kernel,
        out_shape=(
            jax.ShapeDtypeStruct((2, 1, C, W), BF16),
            jax.ShapeDtypeStruct((2, 162, C), F32),
        ),
        in_specs=[any_spec] * 3,
        out_specs=(vmem_spec, vmem_spec),
        scratch_shapes=[
            pltpu.VMEM((C, 5184), BF16),
            pltpu.VMEM((C, 5184), BF16),
            pltpu.VMEM((5184, C), BF16),
            pltpu.VMEM((5184, C), BF16),
            pltpu.VMEM((2, 3, 2, C, W), BF16),
            pltpu.VMEM((2, 3, 2, C, W), BF16),
            pltpu.VMEM((2, 3, 2, C, W), BF16),
            pltpu.VMEM((5184, 2 * W), BF16),
            pltpu.VMEM((3 * C, 2 * W), BF16),
            pltpu.VMEM((3 * C, 2 * W), F32),
            pltpu.VMEM((2, C, W), BF16),
            pltpu.VMEM((2, 5184, W), BF16),
            pltpu.VMEM((2, HALF, W), BF16),
            pltpu.VMEM((2, 2, 2, 6, CHUNK, W), BF16),
            pltpu.VMEM((2, 2, 2, 6, CHUNK, W), BF16),
            pltpu.VMEM((2, 3, 2, 6, 32, W), BF16),
            pltpu.VMEM((2, 3, 6, 64, W), BF16),
            pltpu.VMEM((2, 2, 6, 32, W), BF16),
            pltpu.VMEM((2, 6, 64, W), BF16),
            pltpu.VMEM((2, 3, 6, 16, W), BF16),
            pltpu.VMEM((2, 3, 6, 16, W), BF16),
            pltpu.VMEM((2, 2, 6, 16, W), BF16),
            pltpu.VMEM((2, 7, 2, 16, W), BF16),
            pltpu.VMEM((2, 3, 2, 2, 48, W), BF16),
            pltpu.VMEM((2, 3, 2, 2, 48, W), BF16),
            pltpu.VMEM((2, 4, 2, 2, 48, W), BF16),
            pltpu.VMEM((2, 2, 2, 48, W), BF16),
            pltpu.VMEM((2, 15, 16, W), BF16),
            pltpu.VMEM((2, 8, 3, 16, W), BF16),
            pltpu.VMEM((CHUNK, 2 * W), F32),
            dma((4,)),
            dma((3, 5)),
            dma((3, 2, 3)),
            dma((2, 2, 2, 6)),
            dma((2, 2, 2, 6)),
            dma((2, 2, 3)),
            dma((2, 2, 3)),
            dma((2, 2, 3)),
            dma((2, 2, 3)),
            dma((2, 7)),
            dma((2, 7)),
            dma((2, 3)),
            dma((2, 3)),
            dma((2, 4)),
            dma((2, 4)),
            dma((2, 15)),
            dma((2, 15)),
            dma((2, 7)),
            dma((2, 7)),
        ],
        compiler_params=pltpu.CompilerParams(
            collective_id=0, has_side_effects=True, vmem_limit_bytes=56 * 2**20
        ),
        cost_estimate=pl.CostEstimate(flops=2600000000, bytes_accessed=6000000, transcendentals=500000),
    )(video_in.reshape(2, C, W), jnp.swapaxes(kernels, 1, 2), cotangent.reshape(2, C, W))


def solution(mesh):
    return jax.shard_map(
        on_device,
        mesh=mesh,
        in_specs=(P("tm", "rows", None, None), P(), P("tm", "rows", None, None)),
        out_specs=(P("tm", "rows", None, None), P(None, "rows", None)),
        check_vma=False,
    )
```

```python
import math

import jax
import jax.numpy as jnp
from jax import lax
from jax.experimental import pallas as pl
from jax.experimental.pallas import tpu as pltpu
from jax.sharding import PartitionSpec as P

MESH = pl.DeviceIdType.MESH
F32 = jnp.float32
BF16 = jnp.bfloat16
C = 192
W = 128
TM = 8
ROWS = 32
HALF = 2592
CHUNK = 176


def dot(a, b):
    return lax.dot_general(a, b, (((1,), (0,)), ((), ())), preferred_element_type=F32)


def dot_nt(a, b):
    return lax.dot_general(a, b, (((1,), (1,)), ((), ())), preferred_element_type=F32)


def lane_shift(value, by):
    rolled = pltpu.roll(value, by % W, 1)
    col = lax.broadcasted_iota(jnp.int32, value.shape, 1)
    edge = 0 if by == 1 else W - 1
    return jnp.where(col == edge, 0.0, rolled)


def silu_parts(value):
    sigma = jax.nn.sigmoid(value)
    return value * sigma, sigma * (1.0 + value * (1.0 - sigma))


def chunk_start(j):
    return pl.multiple_of(16 * ((81 * j) // 8), 16)


def kernel(
    video, kernels, cotangent, in_grad, k_grad,
    k1t, k2t, k1, k2, vext, cext, gext, stack, acts2, acc, x1, wa, wb, pair_in, summed,
    r1a, r1b, ta, tb, r2a, r2b, ub, r3, rz1, tz, rz2, tc, rp, r4, final,
    load_sem, halo_send, halo_recv, pair_send, pair_recv,
    s1_send, s1_recv, s2_send, s2_recv, s3_send, s3_recv, z1_send, z1_recv, z2_send, z2_recv,
    p_send, p_recv, s4_send, s4_recv,
):
    t = lax.axis_index("tm")
    r = lax.axis_index("rows")
    xl, y = t // 4, t % 4
    z, xh, c = r // 4, (r // 2) % 2, r % 2
    x = 2 * xh + xl
    has_far = jnp.logical_and(r > 0, r < ROWS - 1)
    far_row, sibling_row = r - 1 + 2 * c, r + 1 - 2 * c
    far_slot, sibling_slot = 2 * c, 2 - 2 * c
    has_past, has_future = t > 0, t < TM - 1

    loads = [
        pltpu.make_async_copy(video, vext.at[1, 1], load_sem.at[0]),
        pltpu.make_async_copy(cotangent, cext.at[0, 1], load_sem.at[1]),
        pltpu.make_async_copy(kernels.at[0], k1t, load_sem.at[2]),
        pltpu.make_async_copy(kernels.at[1], k2t, load_sem.at[3]),
    ]
    for load in loads:
        load.start()

    barrier = pltpu.get_barrier_semaphore()

    def greet(device):
        pl.semaphore_signal(barrier, inc=1, device_id=device, device_id_type=MESH)

    for e in range(1, 8):
        greet((lax.rem(t + e, 8), r))
        greet((t, lax.rem(z + e, 8) * 4 + xh * 2 + c))
    for e in range(8):
        greet((lax.rem(t + e, 8), z * 4 + (1 - xh) * 2 + c))
    greet((t, sibling_row))

    @pl.when(has_far)
    def _():
        greet((t, far_row))

    pl.semaphore_wait(barrier, 23 + jnp.where(has_far, 1, 0))

    exts = (vext, cext, gext)

    def own_of(field):
        return 1 if field == 0 else 0

    def side_of(field):
        return 0 if field == 0 else 1

    def sends_time(field):
        return has_future if field == 0 else has_past

    def gets_time(field):
        return has_past if field == 0 else has_future

    def halo_copy(field, which, f, src=None):
        own, side, ext = own_of(field), side_of(field), exts[field]
        time_device = (t + 1, r) if field == 0 else (t - 1, r)
        if which == 0:
            device, part, row = (t, far_row), own, 2 - 2 * c
        elif which == 1:
            device, part, row = (t, sibling_row), own, 2 * c
        elif which == 2:
            device, part, row = time_device, side, 1
        elif which == 3:
            src, device, part, row = ext.at[own, far_slot], time_device, side, far_slot
        else:
            src, device, part, row = ext.at[side, 1], (t, sibling_row), side, 2 * c
        return pltpu.make_async_remote_copy(
            src_ref=src.at[f],
            dst_ref=ext.at[part, row, f],
            send_sem=halo_send.at[field, which, f],
            recv_sem=halo_recv.at[field, part, row, f],
            device_id=device,
            device_id_type=MESH,
        )

    def sends(field, which):
        return (
            has_far,
            None,
            sends_time(field),
            jnp.logical_and(has_far, sends_time(field)),
            gets_time(field),
        )[which]

    def when(cond, act):
        if cond is None:
            act()
        else:
            pl.when(cond)(act)

    def start_own(field, src):
        for which in (0, 2, 1):
            def act(which=which):
                for f in range(2):
                    halo_copy(field, which, f, src).start()

            when(sends(field, which), act)

    def wait_piece(field, part, row, f):
        pltpu.make_async_remote_copy(
            src_ref=exts[field].at[part, row, f],
            dst_ref=exts[field].at[part, row, f],
            send_sem=halo_send.at[field, 0, f],
            recv_sem=halo_recv.at[field, part, row, f],
            device_id=(t, sibling_row),
            device_id_type=MESH,
        ).wait_recv()

    def wait_slot(field, part, row):
        for f in range(2):
            wait_piece(field, part, row, f)

    def forward(field):
        own, side = own_of(field), side_of(field)
        for f in range(2):
            when(has_far, lambda: wait_piece(field, own, far_slot, f))
            when(sends(field, 3), lambda: halo_copy(field, 3, f).start())
        for f in range(2):
            when(gets_time(field), lambda: wait_piece(field, side, 1, f))
            when(sends(field, 4), lambda: halo_copy(field, 4, f).start())

    def wait_corners(field):
        side = side_of(field)
        when(jnp.logical_and(has_far, gets_time(field)), lambda: wait_slot(field, side, far_slot))
        when(gets_time(field), lambda: wait_slot(field, side, sibling_slot))

    def finish_sends(field, src):
        for which in range(5):
            def act(which=which):
                for f in range(2):
                    halo_copy(field, which, f, src).wait_send()

            when(sends(field, which), act)

    start_own(0, video)
    start_own(1, cotangent)

    zeros_block = jnp.zeros((2, C, W), BF16)

    def clear(field, part, row):
        exts[field][part, row] = zeros_block

    for field in range(3):
        own, side = own_of(field), side_of(field)
        no_time = jnp.logical_not(gets_time(field))
        no_far = jnp.logical_not(has_far)
        when(no_far, lambda: clear(field, own, far_slot))
        when(no_time, lambda: clear(field, side, 1))
        when(no_time, lambda: clear(field, side, sibling_slot))
        when(jnp.logical_or(no_time, no_far), lambda: clear(field, side, far_slot))

    def activate(part, row):
        for f in range(2):
            at = 2 * part + f
            value, _ = silu_parts(vext[part, row, f].astype(F32))
            shifted = (lane_shift(value, 1), value, lane_shift(value, -1))
            for q in range(3):
                block = shifted[q].astype(BF16)
                for to in range(2):
                    tt = at - to
                    if 0 <= tt <= 2:
                        start = (tt * 9 + row * 3 + q) * C
                        stack[start : start + C, to * W : (to + 1) * W] = block

    def turn(src, dst):
        for start in range(0, 5184, W):
            n = min(W, 5184 - start)
            dst[start : start + n, :] = jnp.transpose(src[:, start : start + n])

    def field_pair(ext, tt, p):
        at = (2 - tt, 3 - tt)
        return jnp.concatenate([ext[a // 2, 2 - p, a % 2] for a in at], axis=1)

    EARLY = [(2, 1), (2, 0), (2, 2), (1, 1), (0, 1)]
    LATE = [(1, 0), (1, 2), (0, 0), (0, 2)]

    def back_terms(ext, k_ref, taps, first):
        for tt, p in taps:
            g = tt * 3 + p
            term = dot(k_ref[g * 576 : (g + 1) * 576, :], field_pair(ext, tt, p))
            if first and (tt, p) == taps[0]:
                acc[...] = term
            else:
                acc[...] += term

    def back_sum(f):
        cols = slice(f * W, (f + 1) * W)
        return (
            lane_shift(acc[0:C, cols], -1)
            + acc[C : 2 * C, cols]
            + lane_shift(acc[2 * C : 3 * C, cols], 1)
        )

    loads[0].wait()
    activate(1, 1)
    loads[3].wait()
    turn(k2t, k2)
    loads[2].wait()
    turn(k1t, k1)
    forward(0)
    activate(0, 1)
    wait_slot(0, 1, sibling_slot)
    activate(1, 0)
    activate(1, 2)
    late = dot(k1t[:, 3456:], stack[3456:, :])
    forward(1)
    loads[1].wait()
    wait_slot(1, 0, sibling_slot)
    back_terms(cext, k2, EARLY, True)
    wait_corners(0)
    activate(0, 0)
    activate(0, 2)
    out = late + dot(k1t[:, :3456], stack[:3456, :])
    for f in range(2):
        value = out[:, f * W : (f + 1) * W].astype(BF16)
        x1[f] = value
        value, _ = silu_parts(value.astype(F32))
        shifted = (lane_shift(value, 1), value, lane_shift(value, -1))
        for q in range(3):
            acts2[q * C : (q + 1) * C, f * W : (f + 1) * W] = shifted[q].astype(BF16)

    zeros64 = jnp.zeros((64, 2 * W), BF16)

    def widened(value, upper):
        lo, hi = value[:W], value[W:C]
        return jnp.concatenate([lo, zeros64, hi] if upper else [lo, hi, zeros64], axis=0)

    pair_blocks = []
    for h in range(2):
        for bx in range(2):
            for b in range(6):
                zi, kind = b // 3, b % 3
                z_to = 2 * h + zi + (4 if kind == 2 else 0)
                pair_blocks.append((h, bx, b, kind == 1, 4 * z_to + 2 * bx))

    def steps_of(block):
        j = block[4] % 16
        first = 16 * ((81 * j) // 8)
        last = 16 * ((81 * (j + 1)) // 8) + CHUNK - 1
        return set(range(first // 288, last // 288 + 1))

    def block_src(layer, packed, j):
        ref = wb if packed else wa
        return ref.at[layer, pl.ds(chunk_start(j), CHUNK), :]

    sibling = (t, sibling_row)

    def pair_copy(layer, h, bx, b, packed, j0):
        return pltpu.make_async_remote_copy(
            src_ref=block_src(layer, packed, j0 + 1 - c),
            dst_ref=pair_in.at[layer, h, bx, b],
            send_sem=pair_send.at[layer, h, bx, b],
            recv_sem=pair_recv.at[layer, h, bx, b],
            device_id=sibling,
            device_id_type=MESH,
        )

    def kernel_terms(layer, term, order, done, sent):
        for hg in order:
            k, at = hg % 9, 288 * hg
            value = term(hg, hg >= 9)
            wa[layer, at : at + 288, :] = value[:, :W].astype(BF16)
            rest = value[:, W:].astype(BF16)
            if (hg + 9) % 18 in done:
                wb[layer, 288 * k : 288 * k + 288, :] += rest
            else:
                wb[layer, 288 * k : 288 * k + 288, :] = rest
            done.add(hg)
            for block in pair_blocks:
                if block not in sent and all(n in done and n + 9 in done for n in steps_of(block)):
                    sent.add(block)
                    pair_copy(layer, *block).start()

    def second_term(hg, upper):
        g, part = hg // 2, hg % 2
        pair = widened(field_pair(cext, g // 3, g % 3), upper)
        return dot_nt(acts2[288 * part : 288 * part + 288, :], pair)

    done, sent = set(), set()
    kernel_terms(1, second_term, [9, 12, 3, 13, 14, 15, 16, 17, 8, 2], done, sent)
    wait_corners(1)
    kernel_terms(1, second_term, [0, 1, 10, 11, 4, 5, 6, 7], done, sent)
    back_terms(cext, k2, LATE, False)
    for f in range(2):
        _, slope = silu_parts(x1[f].astype(F32))
        gext[0, 1, f] = (back_sum(f) * slope).astype(BF16)

    def first_term(hg, upper):
        pair = jnp.concatenate([gext[0, 1, 0], gext[0, 1, 1]], axis=1)
        return dot_nt(stack[288 * hg : 288 * hg + 288, :], widened(pair, upper))

    def dev(nxl, ny, nz, nxh):
        return (nxl * 4 + ny, nz * 4 + nxh * 2 + c)

    def remote(src, dst, sems, at, device):
        return pltpu.make_async_remote_copy(
            src_ref=src,
            dst_ref=dst,
            send_sem=sems[0].at[at],
            recv_sem=sems[1].at[at],
            device_id=device,
            device_id_type=MESH,
        )

    def rows_at(start, n):
        return pl.ds(pl.multiple_of(start, 16), n)

    def z_block(nz):
        return (nz % 4) // 2, 3 * (nz % 2) + nz // 4

    def s1_copies(layer):
        out = []
        for d in range(1, 4):
            ny, nx = lax.rem(y + d, 4), lax.rem(x + d, 4)
            src = summed.at[layer, 0, :, :, rows_at(32 * ny, 32), :]
            out.append(remote(src, r1a.at[layer, d - 1], (s1_send, s1_recv), (layer, 0, d - 1), dev(xl, ny, z, xh)))
            src = summed.at[layer, 1, nx // 2, :, rows_at(64 * (nx % 2), 64), :]
            out.append(
                remote(src, r1b.at[layer, d - 1], (s1_send, s1_recv), (layer, 1, d - 1), dev(nx % 2, y, z, nx // 2))
            )
        return out

    def s2_copies(layer):
        out = []
        for d in range(1, 4):
            ny, nx = lax.rem(y + d, 4), lax.rem(x + d, 4)
            src = ta.at[layer, nx // 2, :, rows_at(16 * (nx % 2), 16), :]
            out.append(
                remote(src, r2a.at[layer, d - 1], (s2_send, s2_recv), (layer, 0, d - 1), dev(nx % 2, y, z, nx // 2))
            )
            src = tb.at[layer, :, rows_at(16 * ny, 16), :]
            out.append(remote(src, r2b.at[layer, d - 1], (s2_send, s2_recv), (layer, 1, d - 1), dev(xl, ny, z, xh)))
        return out

    def s3_copies(layer):
        out = []
        for d in range(1, 8):
            nz = lax.rem(z + d, 8)
            nh, nb = z_block(nz)
            src = ub.at[layer, nh, pl.ds(nb, 2)]
            out.append(remote(src, r3.at[layer, d - 1], (s3_send, s3_recv), (layer, d - 1), dev(xl, y, nz, xh)))
        return out

    def z_off(steps):
        return lax.rem(z + steps * (1 - 2 * c) + 8, 8)

    def z_part(layer, nz):
        nh, nb = z_block(nz)
        return summed.at[layer, nh, :, pl.ds(nb, 2), 128:CHUNK, :]

    relays = ((4, 1), (2, 1), (-3, -1))

    def z1_copies(layer):
        out = []
        for k, (to, hop) in enumerate(relays):
            src = z_part(layer, z_off(to))
            out.append(remote(src, rz1.at[layer, k], (z1_send, z1_recv), (layer, k), dev(xl, y, z_off(hop), xh)))
        return out

    def z2_copies(layer):
        out = []
        for k, (to, hop) in enumerate(relays):
            device = dev(xl, y, z_off(to - hop), xh)
            out.append(remote(tz.at[layer, k], rz2.at[layer, k], (z2_send, z2_recv), (layer, k), device))
        src = z_part(layer, z_off(-1))
        out.append(remote(src, rz2.at[layer, 3], (z2_send, z2_recv), (layer, 3), dev(xl, y, z_off(-1), xh)))
        return out

    upper = z // 4
    place = 4 * x + y

    def plane_src(layer, nx, ny):
        return tc.at[layer, nx // 2, lax.rem(upper + nx, 2), rows_at(16 * jnp.minimum(ny, 2), 16), :]

    def plane_copies(layer):
        out = []
        for e in range(1, 16):
            to = lax.rem(place + e, 16)
            nx, ny = to // 4, to % 4
            src = plane_src(layer, nx, ny)
            device = dev(nx % 2, ny, z, nx // 2)
            out.append(remote(src, rp.at[layer, e - 1], (p_send, p_recv), (layer, e - 1), device))
        return out

    def s4_copies(layer):
        out = []
        for e in range(1, 8):
            device = (lax.rem(t + e, 8), r)
            out.append(remote(r4.at[layer, 0], r4.at[layer, e], (s4_send, s4_recv), (layer, e - 1), device))
        return out

    def wide(value):
        return value.astype(F32)

    def start_all(copies):
        for copy in copies:
            copy.start()

    def wait_all(copies):
        for copy in copies:
            copy.wait()

    def stage1(layer):
        copies = s1_copies(layer)
        for half in range(2):
            for h, bx, b, packed, j0 in pair_blocks:
                if h == half:
                    pair_copy(layer, h, bx, b, packed, j0).wait()
                    summed[layer, h, bx, b] = block_src(layer, packed, j0 + c)[...] + pair_in[layer, h, bx, b]
            start_all(copies[half::2])
        start_all(z1_copies(layer))

    def relay(layer):
        wait_all(z1_copies(layer))
        for k, (to, hop) in enumerate(relays):
            own = z_part(layer, z_off(to - hop))[...]
            tz[layer, k] = (wide(own) + wide(rz1[layer, k])).astype(BF16)
        start_all(z2_copies(layer))

    def plane(layer):
        wait_all(z2_copies(layer))
        total = wide(z_part(layer, z)[...])
        for k in range(4):
            total += wide(rz2[layer, k])
        tc[layer] = total.astype(BF16)
        start_all(plane_copies(layer))

    def stage2(layer):
        wait_all(s1_copies(layer))
        own = summed[layer, 0, :, :, rows_at(32 * y, 32), :]
        ta[layer] = (wide(own) + wide(r1a[layer, 0]) + wide(r1a[layer, 1]) + wide(r1a[layer, 2])).astype(BF16)
        own = summed[layer, 1, xh, :, rows_at(64 * xl, 64), :]
        tb[layer] = (wide(own) + wide(r1b[layer, 0]) + wide(r1b[layer, 1]) + wide(r1b[layer, 2])).astype(BF16)
        start_all(s2_copies(layer))

    def stage3(layer):
        wait_all(s2_copies(layer))
        own = ta[layer, xh, :, rows_at(16 * xl, 16), :]
        ub[layer, 0] = (wide(own) + wide(r2a[layer, 0]) + wide(r2a[layer, 1]) + wide(r2a[layer, 2])).astype(BF16)
        own = tb[layer, :, rows_at(16 * y, 16), :]
        ub[layer, 1] = (wide(own) + wide(r2b[layer, 0]) + wide(r2b[layer, 1]) + wide(r2b[layer, 2])).astype(BF16)
        start_all(s3_copies(layer))

    my_half, my_block = z_block(z)
    scale = 1.0 / math.sqrt(TM * 2 * ROWS * W)

    def stage4(layer):
        wait_all(plane_copies(layer))
        total = wide(plane_src(layer, x, y)[...])
        for e in range(15):
            total += wide(rp[layer, e])
        r4[layer, 0, 2] = total.astype(BF16)
        wait_all(s3_copies(layer))
        for k in range(2):
            total = wide(ub[layer, my_half, my_block + k])
            for d in range(7):
                total += wide(r3[layer, d, k])
            r4[layer, 0, k] = total.astype(BF16)
        start_all(s4_copies(layer))

    def unpacked(value):
        return jnp.where(upper == 0, value, pltpu.roll(value, 64, 1))

    def stage5(layer):
        wait_all(s4_copies(layer))
        for e in range(8):
            u = lax.rem(t + 8 - e, 8)
            uy, ux = u % 4, u // 4
            start = jnp.where(my_half == 0, 32 * uy + 16 * ux, 64 * ux + 16 * uy)
            final[rows_at(start, 16), :W] = wide(r4[layer, e, upper]) * scale
            final[rows_at(start, 16), W:] = unpacked(wide(r4[layer, e, 1 - upper]) * scale)
            start = 128 + 16 * jnp.minimum(uy, 2)
            value = wide(r4[layer, e, 2]) * scale

            @pl.when(jnp.logical_and(ux == 0, uy < 3))
            def _(start=start, value=value):
                final[rows_at(start, 16), :W] = value

            @pl.when(jnp.logical_and(ux == 1, uy < 3))
            def _(start=start, value=value):
                final[rows_at(start, 16), W:] = unpacked(value)

        off = 4 * (z % 2) + 2 * xh + c
        for k in range(8):
            @pl.when(off == k)
            def _(k=k):
                k_grad[layer] = final[2 * k : 2 * k + 162, :C]

    stage1(1)
    kernel_terms(0, first_term, [n for k in range(9) for n in (k, k + 9)], set(), set())
    stage1(0)
    start_own(2, gext.at[0, 1])
    relay(1)
    stage2(1)
    relay(0)
    stage2(0)
    plane(1)
    stage3(1)
    forward(2)
    plane(0)
    stage3(0)
    wait_slot(2, 0, sibling_slot)
    back_terms(gext, k1, EARLY, True)
    stage4(1)
    wait_corners(2)
    back_terms(gext, k1, LATE, False)
    for f in range(2):
        _, slope = silu_parts(vext[1, 1, f].astype(F32))
        in_grad[f, 0] = (back_sum(f) * slope).astype(BF16)

    stage4(0)
    stage5(1)
    stage5(0)

    finish_sends(0, video)
    finish_sends(1, cotangent)
    finish_sends(2, gext.at[0, 1])


def on_device(video_in, kernels, cotangent):
    dma = pltpu.SemaphoreType.DMA
    any_spec = pl.BlockSpec(memory_space=pl.ANY)
    vmem_spec = pl.BlockSpec(memory_space=pltpu.VMEM)
    return pl.pallas_call(
        kernel,
        out_shape=(
            jax.ShapeDtypeStruct((2, 1, C, W), BF16),
            jax.ShapeDtypeStruct((2, 162, C), F32),
        ),
        in_specs=[any_spec] * 3,
        out_specs=(vmem_spec, vmem_spec),
        scratch_shapes=[
            pltpu.VMEM((C, 5184), BF16),
            pltpu.VMEM((C, 5184), BF16),
            pltpu.VMEM((5184, C), BF16),
            pltpu.VMEM((5184, C), BF16),
            pltpu.VMEM((2, 3, 2, C, W), BF16),
            pltpu.VMEM((2, 3, 2, C, W), BF16),
            pltpu.VMEM((2, 3, 2, C, W), BF16),
            pltpu.VMEM((5184, 2 * W), BF16),
            pltpu.VMEM((3 * C, 2 * W), BF16),
            pltpu.VMEM((3 * C, 2 * W), F32),
            pltpu.VMEM((2, C, W), BF16),
            pltpu.VMEM((2, 5184, W), BF16),
            pltpu.VMEM((2, HALF, W), BF16),
            pltpu.VMEM((2, 2, 2, 6, CHUNK, W), BF16),
            pltpu.VMEM((2, 2, 2, 6, CHUNK, W), BF16),
            pltpu.VMEM((2, 3, 2, 6, 32, W), BF16),
            pltpu.VMEM((2, 3, 6, 64, W), BF16),
            pltpu.VMEM((2, 2, 6, 32, W), BF16),
            pltpu.VMEM((2, 6, 64, W), BF16),
            pltpu.VMEM((2, 3, 6, 16, W), BF16),
            pltpu.VMEM((2, 3, 6, 16, W), BF16),
            pltpu.VMEM((2, 2, 6, 16, W), BF16),
            pltpu.VMEM((2, 7, 2, 16, W), BF16),
            pltpu.VMEM((2, 3, 2, 2, 48, W), BF16),
            pltpu.VMEM((2, 3, 2, 2, 48, W), BF16),
            pltpu.VMEM((2, 4, 2, 2, 48, W), BF16),
            pltpu.VMEM((2, 2, 2, 48, W), BF16),
            pltpu.VMEM((2, 15, 16, W), BF16),
            pltpu.VMEM((2, 8, 3, 16, W), BF16),
            pltpu.VMEM((CHUNK, 2 * W), F32),
            dma((4,)),
            dma((3, 5, 2)),
            dma((3, 2, 3, 2)),
            dma((2, 2, 2, 6)),
            dma((2, 2, 2, 6)),
            dma((2, 2, 3)),
            dma((2, 2, 3)),
            dma((2, 2, 3)),
            dma((2, 2, 3)),
            dma((2, 7)),
            dma((2, 7)),
            dma((2, 3)),
            dma((2, 3)),
            dma((2, 4)),
            dma((2, 4)),
            dma((2, 15)),
            dma((2, 15)),
            dma((2, 7)),
            dma((2, 7)),
        ],
        compiler_params=pltpu.CompilerParams(
            collective_id=0, has_side_effects=True, vmem_limit_bytes=56 * 2**20
        ),
        cost_estimate=pl.CostEstimate(flops=2600000000, bytes_accessed=6000000, transcendentals=500000),
    )(video_in.reshape(2, C, W), jnp.swapaxes(kernels, 1, 2), cotangent.reshape(2, C, W))


def solution(mesh):
    return jax.shard_map(
        on_device,
        mesh=mesh,
        in_specs=(P("tm", "rows", None, None), P(), P("tm", "rows", None, None)),
        out_specs=(P("tm", "rows", None, None), P(None, "rows", None)),
        check_vma=False,
    )
```

```python
import math

import jax
import jax.numpy as jnp
from jax import lax
from jax.experimental import pallas as pl
from jax.experimental.pallas import tpu as pltpu
from jax.sharding import PartitionSpec as P

MESH = pl.DeviceIdType.MESH
F32 = jnp.float32
BF16 = jnp.bfloat16
C = 192
W = 128
TM = 8
ROWS = 32
CHUNK = 176


def dot(a, b):
    return lax.dot_general(a, b, (((1,), (0,)), ((), ())), preferred_element_type=F32)


def dot_nt(a, b):
    return lax.dot_general(a, b, (((1,), (1,)), ((), ())), preferred_element_type=F32)


def lane_shift(value, by):
    rolled = pltpu.roll(value, by % W, 1)
    col = lax.broadcasted_iota(jnp.int32, value.shape, 1)
    edge = 0 if by == 1 else W - 1
    return jnp.where(col == edge, 0.0, rolled)


def silu_parts(value):
    sigma = jax.nn.sigmoid(value)
    return value * sigma, sigma * (1.0 + value * (1.0 - sigma))


def chunk_start(j):
    return pl.multiple_of(16 * ((81 * j) // 8), 16)


def kernel(
    video, kernels, cotangent, in_grad, k_grad,
    k1t, k2t, k1, k2, vext, cext, gext, stack, a2, acts2, acc, x1, summed,
    r1a, r1b, ta, tb, r2a, r2b, ub, r3, rz1, tz, rz2, tc, rp, r4, final,
    load_sem, halo_send, halo_recv, a2_sem,
    s1_send, s1_recv, s2_send, s2_recv, s3_send, s3_recv, z1_send, z1_recv, z2_send, z2_recv,
    p_send, p_recv, s4_send, s4_recv,
):
    t = lax.axis_index("tm")
    r = lax.axis_index("rows")
    xl, y = t // 4, t % 4
    z, xh, c = r // 4, (r // 2) % 2, r % 2
    x = 2 * xh + xl
    has_far = jnp.logical_and(r > 0, r < ROWS - 1)
    far_row, sibling_row = r - 1 + 2 * c, r + 1 - 2 * c
    me, sib, far, sib_far = 1 + c, 2 - c, 3 * c, 3 - 3 * c
    sib_has_far = jnp.logical_and(sibling_row > 0, sibling_row < ROWS - 1)
    has_past, has_future = t > 0, t < TM - 1

    loads = [
        pltpu.make_async_copy(video, vext.at[1, me], load_sem.at[0]),
        pltpu.make_async_copy(cotangent, cext.at[0, me], load_sem.at[1]),
        pltpu.make_async_copy(kernels.at[0], k1t, load_sem.at[2]),
        pltpu.make_async_copy(kernels.at[1], k2t, load_sem.at[3]),
    ]
    for load in loads:
        load.start()

    barrier = pltpu.get_barrier_semaphore()

    def greet(device):
        pl.semaphore_signal(barrier, inc=1, device_id=device, device_id_type=MESH)

    for e in range(1, 8):
        greet((lax.rem(t + e, 8), r))
        greet((t, lax.rem(z + e, 8) * 4 + xh * 2 + c))
    for e in range(8):
        greet((lax.rem(t + e, 8), z * 4 + (1 - xh) * 2 + c))
    greet((t, sibling_row))

    @pl.when(has_far)
    def _():
        greet((t, far_row))

    pl.semaphore_wait(barrier, 23 + jnp.where(has_far, 1, 0))

    exts = (vext, cext, gext)

    def own_of(field):
        return 1 if field == 0 else 0

    def side_of(field):
        return 0 if field == 0 else 1

    def sends_time(field):
        return has_future if field == 0 else has_past

    def gets_time(field):
        return has_past if field == 0 else has_future

    def halo_copy(field, which, f, src=None):
        own, side, ext = own_of(field), side_of(field), exts[field]
        time_device = (t + 1, r) if field == 0 else (t - 1, r)
        part, row, device = (
            (own, sib_far, (t, far_row)),
            (own, me, (t, sibling_row)),
            (side, me, time_device),
            (side, far, time_device),
            (side, me, (t, sibling_row)),
            (own, far, (t, sibling_row)),
            (side, far, (t, sibling_row)),
        )[which]
        if which == 3:
            src = ext.at[own, far]
        elif which > 3:
            src = ext.at[part, row]
        return pltpu.make_async_remote_copy(
            src_ref=src.at[f],
            dst_ref=ext.at[part, row, f],
            send_sem=halo_send.at[field, which, f],
            recv_sem=halo_recv.at[field, part, row, f],
            device_id=device,
            device_id_type=MESH,
        )

    def sends(field, which):
        return (
            has_far,
            None,
            sends_time(field),
            jnp.logical_and(has_far, sends_time(field)),
            gets_time(field),
            has_far,
            jnp.logical_and(has_far, gets_time(field)),
        )[which]

    def when(cond, act):
        if cond is None:
            act()
        else:
            pl.when(cond)(act)

    def start_halo(field, which, src=None):
        def act():
            for f in range(2):
                halo_copy(field, which, f, src).start()

        when(sends(field, which), act)

    def start_own(field, src):
        for which in (0, 2, 1):
            start_halo(field, which, src)

    def wait_piece(field, part, row, f):
        pltpu.make_async_remote_copy(
            src_ref=exts[field].at[part, row, f],
            dst_ref=exts[field].at[part, row, f],
            send_sem=halo_send.at[field, 0, f],
            recv_sem=halo_recv.at[field, part, row, f],
            device_id=(t, sibling_row),
            device_id_type=MESH,
        ).wait_recv()

    def wait_block(field, part, row, cond=None):
        def act():
            for f in range(2):
                wait_piece(field, part, row, f)

        when(cond, act)

    def forward(field):
        own, side = own_of(field), side_of(field)
        for f in range(2):
            when(has_far, lambda: wait_piece(field, own, far, f))
            when(sends(field, 3), lambda: halo_copy(field, 3, f).start())
        if field < 2:
            start_halo(field, 5)
        for f in range(2):
            when(gets_time(field), lambda: wait_piece(field, side, me, f))
            when(sends(field, 4), lambda: halo_copy(field, 4, f).start())

    def wait_sibling(field):
        wait_block(field, own_of(field), sib)

    def wait_corners(field):
        side = side_of(field)
        wait_block(field, side, far, jnp.logical_and(has_far, gets_time(field)))
        if field < 2:
            start_halo(field, 6)
        wait_block(field, side, sib, gets_time(field))

    def wait_sibling_far(field, corner):
        if corner:
            wait_block(field, side_of(field), sib_far, jnp.logical_and(sib_has_far, gets_time(field)))
        else:
            wait_block(field, own_of(field), sib_far, sib_has_far)

    def finish_sends(field, src):
        for which in range(7 if field < 2 else 5):
            def act(which=which):
                for f in range(2):
                    halo_copy(field, which, f, src).wait_send()

            when(sends(field, which), act)

    start_own(0, video)
    start_own(1, cotangent)

    zeros_block = jnp.zeros((2, C, W), BF16)

    def clear(field, part, row):
        exts[field][part, row] = zeros_block

    for field in range(3):
        own, side = own_of(field), side_of(field)
        no_time = jnp.logical_not(gets_time(field))
        for row, has in ((far, has_far), (sib_far, sib_has_far)):
            none = jnp.logical_not(has)
            when(none, lambda: clear(field, own, row))
            when(jnp.logical_or(no_time, none), lambda: clear(field, side, row))
        for row in (me, sib):
            when(no_time, lambda: clear(field, side, row))

    enters = {
        "me": (me, ((c, 1), (1 - c, 2 * c))),
        "sib": (sib, ((c, 2 - 2 * c), (1 - c, 1))),
        "far": (far, ((c, 2 * c),)),
        "sib_far": (sib_far, ((1 - c, 2 - 2 * c),)),
    }

    def activate(part, name):
        row, targets = enters[name]
        for f in range(2):
            at = 2 * part + f
            value, _ = silu_parts(vext[part, row, f].astype(F32))
            shifted = (lane_shift(value, 1), value, lane_shift(value, -1))
            for q in range(3):
                block = shifted[q].astype(BF16)
                for to in range(2):
                    tt = at - to
                    if 0 <= tt <= 2:
                        for center, p in targets:
                            start = pl.multiple_of((tt * 9 + q) * C + p * 3 * C, 16)
                            stack[center, pl.ds(start, C), to * W : (to + 1) * W] = block

    def turn(src, dst):
        for start in range(0, 5184, W):
            n = min(W, 5184 - start)
            dst[start : start + n, :] = jnp.transpose(src[:, start : start + n])

    def field_pair(ext, tt, p, center):
        at = (2 - tt, 3 - tt)
        return jnp.concatenate([ext[a // 2, center + 1 - p, a % 2] for a in at], axis=1)

    EARLY = [(2, 1), (2, 0), (2, 2), (1, 1), (0, 1)]
    LATE = [(1, 0), (1, 2), (0, 0), (0, 2)]

    def back_terms(ext, k_ref, taps, first):
        for tt, p in taps:
            g = tt * 3 + p
            term = dot(k_ref[g * 576 : (g + 1) * 576, :], field_pair(ext, tt, p, me))
            if first and (tt, p) == taps[0]:
                acc[...] = term
            else:
                acc[...] += term

    def back_sum(f):
        cols = slice(f * W, (f + 1) * W)
        return (
            lane_shift(acc[0:C, cols], -1)
            + acc[C : 2 * C, cols]
            + lane_shift(acc[2 * C : 3 * C, cols], 1)
        )

    zeros64 = jnp.zeros((64, 2 * W), BF16)

    def widened(value, upper):
        lo, hi = value[:W], value[W:C]
        return jnp.concatenate([lo, zeros64, hi] if upper else [lo, hi, zeros64], axis=0)

    def put(layer, m, bx, low, high):
        h, b = m // 2, 3 * (m % 2)
        summed[layer, h, bx, b] = low[:, :W].astype(BF16)
        summed[layer, h, bx, b + 1] = (low[:, W:] + high[:, W:]).astype(BF16)
        summed[layer, h, bx, b + 2] = high[:, :W].astype(BF16)

    def second_chunk(j, upper):
        start, pieces = 16 * ((81 * j) // 8), []
        at = start
        while at < start + CHUNK:
            g = at // 576
            n = min(start + CHUNK, 576 * (g + 1)) - at
            rhs = [widened(field_pair(cext, g // 3, g % 3, center), upper) for center in (1, 2)]
            pieces.append(dot_nt(acts2[at - 576 * g : at - 576 * g + n, :], jnp.concatenate(rhs, axis=1)))
            at += n
        return pieces[0] if len(pieces) == 1 else jnp.concatenate(pieces, axis=0)

    def second_terms(planes):
        for core in range(2):
            @pl.when(c == core)
            def _(core=core):
                for m in planes:
                    for bx in range(2):
                        j = 8 * m + 2 * bx + core
                        put(1, m, bx, second_chunk(j, False), second_chunk(j + 4, True))

    def first_terms(planes):
        rows = [jnp.concatenate([gext[0, center, 0], gext[0, center, 1]], axis=1) for center in (1, 2)]
        rhs = [jnp.concatenate([widened(v, upper) for v in rows], axis=1) for upper in (False, True)]
        for m in planes:
            for bx in range(2):
                out = []
                for upper in range(2):
                    at = pl.ds(chunk_start(8 * m + 4 * upper + 2 * bx + c), CHUNK)
                    out.append(dot_nt(jnp.concatenate([stack[0, at, :], stack[1, at, :]], axis=1), rhs[upper]))
                put(0, m, bx, *out)

    loads[0].wait()
    activate(1, "me")
    loads[3].wait()
    turn(k2t, k2)
    loads[2].wait()
    turn(k1t, k1)
    forward(0)
    activate(0, "me")
    activate(1, "far")
    wait_sibling(0)
    activate(1, "sib")
    late = dot(k1t[:, 3456:], stack[c, 3456:, :])
    forward(1)
    loads[1].wait()
    wait_sibling(1)
    back_terms(cext, k2, EARLY, True)
    wait_corners(0)
    activate(0, "far")
    activate(0, "sib")
    out = late + dot(k1t[:, :3456], stack[c, :3456, :])
    for f in range(2):
        value = out[:, f * W : (f + 1) * W].astype(BF16)
        x1[f] = value
        value, _ = silu_parts(value.astype(F32))
        a2[c, f] = value.astype(BF16)
    a2_copy = pltpu.make_async_remote_copy(
        src_ref=a2.at[c],
        dst_ref=a2.at[c],
        send_sem=a2_sem.at[0],
        recv_sem=a2_sem.at[1],
        device_id=(t, sibling_row),
        device_id_type=MESH,
    )
    a2_copy.start()
    wait_sibling_far(0, False)
    activate(1, "sib_far")
    wait_sibling_far(1, False)
    a2_copy.wait_recv()
    for center in range(2):
        for f in range(2):
            value = a2[center, f].astype(F32)
            shifted = (lane_shift(value, 1), value, lane_shift(value, -1))
            cols = slice((2 * center + f) * W, (2 * center + f + 1) * W)
            for q in range(3):
                acts2[q * C : (q + 1) * C, cols] = shifted[q].astype(BF16)
    second_terms([3])
    wait_corners(1)
    back_terms(cext, k2, LATE, False)
    for f in range(2):
        _, slope = silu_parts(x1[f].astype(F32))
        gext[0, me, f] = (back_sum(f) * slope).astype(BF16)
    start_halo(2, 1, gext.at[0, me])
    wait_sibling_far(1, True)
    second_terms([2, 0, 1])

    def dev(nxl, ny, nz, nxh):
        return (nxl * 4 + ny, nz * 4 + nxh * 2 + c)

    def remote(src, dst, sems, at, device):
        return pltpu.make_async_remote_copy(
            src_ref=src,
            dst_ref=dst,
            send_sem=sems[0].at[at],
            recv_sem=sems[1].at[at],
            device_id=device,
            device_id_type=MESH,
        )

    def rows_at(start, n):
        return pl.ds(pl.multiple_of(start, 16), n)

    def z_block(nz):
        return nz // 4, 3 * ((nz // 2) % 2) + nz % 2

    def s1_copies(layer):
        out = []
        for d in range(1, 4):
            ny, nx = lax.rem(y + d, 4), lax.rem(x + d, 4)
            src = summed.at[layer, 0, :, :, rows_at(32 * ny, 32), :]
            out.append(remote(src, r1a.at[layer, d - 1], (s1_send, s1_recv), (layer, 0, d - 1), dev(xl, ny, z, xh)))
            src = summed.at[layer, 1, nx // 2, :, rows_at(64 * (nx % 2), 64), :]
            out.append(
                remote(src, r1b.at[layer, d - 1], (s1_send, s1_recv), (layer, 1, d - 1), dev(nx % 2, y, z, nx // 2))
            )
        return out

    def s2_copies(layer):
        out = []
        for d in range(1, 4):
            ny, nx = lax.rem(y + d, 4), lax.rem(x + d, 4)
            src = ta.at[layer, nx // 2, :, rows_at(16 * (nx % 2), 16), :]
            out.append(
                remote(src, r2a.at[layer, d - 1], (s2_send, s2_recv), (layer, 0, d - 1), dev(nx % 2, y, z, nx // 2))
            )
            src = tb.at[layer, :, rows_at(16 * ny, 16), :]
            out.append(remote(src, r2b.at[layer, d - 1], (s2_send, s2_recv), (layer, 1, d - 1), dev(xl, ny, z, xh)))
        return out

    def s3_copies(layer):
        out = []
        for d in range(1, 8):
            nz = lax.rem(z + d, 8)
            nh, nb = z_block(nz)
            src = ub.at[layer, nh, pl.ds(nb, 2)]
            out.append(remote(src, r3.at[layer, d - 1], (s3_send, s3_recv), (layer, d - 1), dev(xl, y, nz, xh)))
        return out

    def z_off(steps):
        return lax.rem(z + steps * (1 - 2 * c) + 8, 8)

    def z_part(layer, nz):
        nh, nb = z_block(nz)
        return summed.at[layer, nh, :, pl.ds(nb, 2), 128:CHUNK, :]

    relays = ((4, 1), (2, 1), (-3, -1))

    def z1_copies(layer):
        out = []
        for k, (to, hop) in enumerate(relays):
            src = z_part(layer, z_off(to))
            out.append(remote(src, rz1.at[layer, k], (z1_send, z1_recv), (layer, k), dev(xl, y, z_off(hop), xh)))
        return out

    def z2_copies(layer):
        out = []
        for k, (to, hop) in enumerate(relays):
            device = dev(xl, y, z_off(to - hop), xh)
            out.append(remote(tz.at[layer, k], rz2.at[layer, k], (z2_send, z2_recv), (layer, k), device))
        src = z_part(layer, z_off(-1))
        out.append(remote(src, rz2.at[layer, 3], (z2_send, z2_recv), (layer, 3), dev(xl, y, z_off(-1), xh)))
        return out

    upper = z % 2
    place = 4 * x + y

    def plane_src(layer, nx, ny):
        return tc.at[layer, nx // 2, lax.rem(upper + nx, 2), rows_at(16 * jnp.minimum(ny, 2), 16), :]

    def plane_copies(layer):
        out = []
        for e in range(1, 16):
            to = lax.rem(place + e, 16)
            nx, ny = to // 4, to % 4
            src = plane_src(layer, nx, ny)
            device = dev(nx % 2, ny, z, nx // 2)
            out.append(remote(src, rp.at[layer, e - 1], (p_send, p_recv), (layer, e - 1), device))
        return out

    def s4_copies(layer):
        out = []
        for e in range(1, 8):
            device = (lax.rem(t + e, 8), r)
            out.append(remote(r4.at[layer, 0], r4.at[layer, e], (s4_send, s4_recv), (layer, e - 1), device))
        return out

    def wide(value):
        return value.astype(F32)

    def start_all(copies):
        for copy in copies:
            copy.start()

    def wait_all(copies):
        for copy in copies:
            copy.wait()

    def stage1(layer):
        start_all(s1_copies(layer))
        start_all(z1_copies(layer))

    def relay(layer):
        wait_all(z1_copies(layer))
        for k, (to, hop) in enumerate(relays):
            own = z_part(layer, z_off(to - hop))[...]
            tz[layer, k] = (wide(own) + wide(rz1[layer, k])).astype(BF16)
        start_all(z2_copies(layer))

    def plane(layer):
        wait_all(z2_copies(layer))
        total = wide(z_part(layer, z)[...])
        for k in range(4):
            total += wide(rz2[layer, k])
        tc[layer] = total.astype(BF16)
        start_all(plane_copies(layer))

    def stage2(layer):
        wait_all(s1_copies(layer))
        own = summed[layer, 0, :, :, rows_at(32 * y, 32), :]
        ta[layer] = (wide(own) + wide(r1a[layer, 0]) + wide(r1a[layer, 1]) + wide(r1a[layer, 2])).astype(BF16)
        own = summed[layer, 1, xh, :, rows_at(64 * xl, 64), :]
        tb[layer] = (wide(own) + wide(r1b[layer, 0]) + wide(r1b[layer, 1]) + wide(r1b[layer, 2])).astype(BF16)
        start_all(s2_copies(layer))

    def stage3(layer):
        wait_all(s2_copies(layer))
        own = ta[layer, xh, :, rows_at(16 * xl, 16), :]
        ub[layer, 0] = (wide(own) + wide(r2a[layer, 0]) + wide(r2a[layer, 1]) + wide(r2a[layer, 2])).astype(BF16)
        own = tb[layer, :, rows_at(16 * y, 16), :]
        ub[layer, 1] = (wide(own) + wide(r2b[layer, 0]) + wide(r2b[layer, 1]) + wide(r2b[layer, 2])).astype(BF16)
        start_all(s3_copies(layer))

    my_half, my_block = z_block(z)
    scale = 1.0 / math.sqrt(TM * 2 * ROWS * W)

    def stage4(layer):
        wait_all(plane_copies(layer))
        total = wide(plane_src(layer, x, y)[...])
        for e in range(15):
            total += wide(rp[layer, e])
        r4[layer, 0, 2] = total.astype(BF16)
        wait_all(s3_copies(layer))
        for k in range(2):
            total = wide(ub[layer, my_half, my_block + k])
            for d in range(7):
                total += wide(r3[layer, d, k])
            r4[layer, 0, k] = total.astype(BF16)
        start_all(s4_copies(layer))

    def unpacked(value):
        return jnp.where(upper == 0, value, pltpu.roll(value, 64, 1))

    def stage5(layer):
        wait_all(s4_copies(layer))
        for e in range(8):
            u = lax.rem(t + 8 - e, 8)
            uy, ux = u % 4, u // 4
            start = jnp.where(my_half == 0, 32 * uy + 16 * ux, 64 * ux + 16 * uy)
            final[rows_at(start, 16), :W] = wide(r4[layer, e, upper]) * scale
            final[rows_at(start, 16), W:] = unpacked(wide(r4[layer, e, 1 - upper]) * scale)
            start = 128 + 16 * jnp.minimum(uy, 2)
            value = wide(r4[layer, e, 2]) * scale

            @pl.when(jnp.logical_and(ux == 0, uy < 3))
            def _(start=start, value=value):
                final[rows_at(start, 16), :W] = value

            @pl.when(jnp.logical_and(ux == 1, uy < 3))
            def _(start=start, value=value):
                final[rows_at(start, 16), W:] = unpacked(value)

        off = 4 * (z % 2) + 2 * xh + c
        for k in range(8):
            @pl.when(off == k)
            def _(k=k):
                k_grad[layer] = final[2 * k : 2 * k + 162, :C]

    stage1(1)
    wait_sibling_far(0, True)
    activate(0, "sib_far")
    wait_sibling(2)
    first_terms(range(4))
    stage1(0)
    start_halo(2, 0, gext.at[0, me])
    start_halo(2, 2, gext.at[0, me])
    relay(1)
    stage2(1)
    relay(0)
    stage2(0)
    plane(1)
    stage3(1)
    forward(2)
    plane(0)
    stage3(0)
    back_terms(gext, k1, EARLY, True)
    stage4(1)
    wait_corners(2)
    back_terms(gext, k1, LATE, False)
    for f in range(2):
        _, slope = silu_parts(vext[1, me, f].astype(F32))
        in_grad[f, 0] = (back_sum(f) * slope).astype(BF16)

    stage4(0)
    stage5(1)
    stage5(0)

    finish_sends(0, video)
    finish_sends(1, cotangent)
    finish_sends(2, gext.at[0, me])
    a2_copy.wait_send()


def finish(in_src, k_src, in_dst, k_dst):
    in_dst[:, 0] = in_src[:, 0]
    for layer in range(2):
        k_dst[:, layer, :] = k_src[layer]


def on_device(video_in, kernels, cotangent):
    dma = pltpu.SemaphoreType.DMA
    any_spec = pl.BlockSpec(memory_space=pl.ANY)
    vmem_spec = pl.BlockSpec(memory_space=pltpu.VMEM)
    in_grad, k_grad = pl.pallas_call(
        kernel,
        out_shape=(
            jax.ShapeDtypeStruct((2, 1, C, W), BF16),
            jax.ShapeDtypeStruct((2, 162, C), F32),
        ),
        in_specs=[any_spec] * 3,
        out_specs=(vmem_spec, vmem_spec),
        scratch_shapes=[
            pltpu.VMEM((C, 5184), BF16),
            pltpu.VMEM((C, 5184), BF16),
            pltpu.VMEM((5184, C), BF16),
            pltpu.VMEM((5184, C), BF16),
            pltpu.VMEM((2, 4, 2, C, W), BF16),
            pltpu.VMEM((2, 4, 2, C, W), BF16),
            pltpu.VMEM((2, 4, 2, C, W), BF16),
            pltpu.VMEM((2, 5184, 2 * W), BF16),
            pltpu.VMEM((2, 2, C, W), BF16),
            pltpu.VMEM((3 * C, 4 * W), BF16),
            pltpu.VMEM((3 * C, 2 * W), F32),
            pltpu.VMEM((2, C, W), BF16),
            pltpu.VMEM((2, 2, 2, 6, CHUNK, W), BF16),
            pltpu.VMEM((2, 3, 2, 6, 32, W), BF16),
            pltpu.VMEM((2, 3, 6, 64, W), BF16),
            pltpu.VMEM((2, 2, 6, 32, W), BF16),
            pltpu.VMEM((2, 6, 64, W), BF16),
            pltpu.VMEM((2, 3, 6, 16, W), BF16),
            pltpu.VMEM((2, 3, 6, 16, W), BF16),
            pltpu.VMEM((2, 2, 6, 16, W), BF16),
            pltpu.VMEM((2, 7, 2, 16, W), BF16),
            pltpu.VMEM((2, 3, 2, 2, 48, W), BF16),
            pltpu.VMEM((2, 3, 2, 2, 48, W), BF16),
            pltpu.VMEM((2, 4, 2, 2, 48, W), BF16),
            pltpu.VMEM((2, 2, 2, 48, W), BF16),
            pltpu.VMEM((2, 15, 16, W), BF16),
            pltpu.VMEM((2, 8, 3, 16, W), BF16),
            pltpu.VMEM((CHUNK, 2 * W), F32),
            dma((4,)),
            dma((3, 7, 2)),
            dma((3, 2, 4, 2)),
            dma((2,)),
            dma((2, 2, 3)),
            dma((2, 2, 3)),
            dma((2, 2, 3)),
            dma((2, 2, 3)),
            dma((2, 7)),
            dma((2, 7)),
            dma((2, 3)),
            dma((2, 3)),
            dma((2, 4)),
            dma((2, 4)),
            dma((2, 15)),
            dma((2, 15)),
            dma((2, 7)),
            dma((2, 7)),
        ],
        compiler_params=pltpu.CompilerParams(
            collective_id=0, has_side_effects=True, vmem_limit_bytes=56 * 2**20
        ),
        cost_estimate=pl.CostEstimate(flops=2600000000, bytes_accessed=6000000, transcendentals=500000),
    )(video_in.reshape(2, C, W), jnp.swapaxes(kernels, 1, 2), cotangent.reshape(2, C, W))
    in_grad, k_grad = pl.pallas_call(
        finish,
        out_shape=(
            jax.ShapeDtypeStruct((2, 1, C, W), BF16),
            jax.ShapeDtypeStruct((162, 2, C), F32),
        ),
        in_specs=[vmem_spec, vmem_spec],
        out_specs=(vmem_spec, vmem_spec),
    )(in_grad, k_grad)
    return in_grad, jnp.swapaxes(k_grad, 0, 1)


def solution(mesh):
    return jax.shard_map(
        on_device,
        mesh=mesh,
        in_specs=(P("tm", "rows", None, None), P(), P("tm", "rows", None, None)),
        out_specs=(P("tm", "rows", None, None), P(None, "rows", None)),
        check_vma=False,
    )
```

```python
import math

import jax
import jax.numpy as jnp
from jax import lax
from jax.experimental import pallas as pl
from jax.experimental.pallas import tpu as pltpu
from jax.sharding import PartitionSpec as P

MESH = pl.DeviceIdType.MESH
F32 = jnp.float32
BF16 = jnp.bfloat16
C = 192
W = 128
TM = 8
ROWS = 32
CHUNK = 176


def dot(a, b):
    return lax.dot_general(a, b, (((1,), (0,)), ((), ())), preferred_element_type=F32)


def dot_nt(a, b):
    return lax.dot_general(a, b, (((1,), (1,)), ((), ())), preferred_element_type=F32)


def lane_shift(value, by):
    rolled = pltpu.roll(value, by % W, 1)
    col = lax.broadcasted_iota(jnp.int32, value.shape, 1)
    edge = 0 if by == 1 else W - 1
    return jnp.where(col == edge, 0.0, rolled)


def silu_parts(value):
    sigma = jax.nn.sigmoid(value)
    return value * sigma, sigma * (1.0 + value * (1.0 - sigma))


def chunk_start(j):
    return pl.multiple_of(16 * ((81 * j) // 8), 16)


def kernel(
    video, kernels, cotangent, in_grad, k_grad,
    k1t, k2t, k1, k2, vext, cext, gext, stack, a2, acts2, acc, x1, summed,
    r1a, r1b, ta, tb, r2a, r2b, ub, r3, rz1, tz, rz2, tc, rp, r4, final,
    load_sem, halo_send, halo_recv, a2_sem,
    s1_send, s1_recv, s2_send, s2_recv, s3_send, s3_recv, z1_send, z1_recv, z2_send, z2_recv,
    p_send, p_recv, s4_send, s4_recv,
):
    t = lax.axis_index("tm")
    r = lax.axis_index("rows")
    xl, y = t // 4, t % 4
    z, xh, c = r // 4, (r // 2) % 2, r % 2
    x = 2 * xh + xl
    has_far = jnp.logical_and(r > 0, r < ROWS - 1)
    far_row, sibling_row = r - 1 + 2 * c, r + 1 - 2 * c
    me, sib, far, sib_far = 1 + c, 2 - c, 3 * c, 3 - 3 * c
    sib_has_far = jnp.logical_and(sibling_row > 0, sibling_row < ROWS - 1)
    has_past, has_future = t > 0, t < TM - 1

    loads = [
        pltpu.make_async_copy(video, vext.at[1, me], load_sem.at[0]),
        pltpu.make_async_copy(cotangent, cext.at[0, me], load_sem.at[1]),
        pltpu.make_async_copy(kernels.at[0], k1t, load_sem.at[2]),
        pltpu.make_async_copy(kernels.at[1], k2t, load_sem.at[3]),
    ]
    for load in loads:
        load.start()

    barrier = pltpu.get_barrier_semaphore()

    def greet(device):
        pl.semaphore_signal(barrier, inc=1, device_id=device, device_id_type=MESH)

    for e in range(1, 8):
        greet((lax.rem(t + e, 8), r))
        greet((t, lax.rem(z + e, 8) * 4 + xh * 2 + c))
    for e in range(8):
        greet((lax.rem(t + e, 8), z * 4 + (1 - xh) * 2 + c))
    greet((t, sibling_row))

    @pl.when(has_far)
    def _():
        greet((t, far_row))

    pl.semaphore_wait(barrier, 23 + jnp.where(has_far, 1, 0))

    exts = (vext, cext, gext)

    def own_of(field):
        return 1 if field == 0 else 0

    def side_of(field):
        return 0 if field == 0 else 1

    def sends_time(field):
        return has_future if field == 0 else has_past

    def gets_time(field):
        return has_past if field == 0 else has_future

    def halo_copy(field, which, f, src=None):
        own, side, ext = own_of(field), side_of(field), exts[field]
        time_device = (t + 1, r) if field == 0 else (t - 1, r)
        part, row, device = (
            (own, sib_far, (t, far_row)),
            (own, me, (t, sibling_row)),
            (side, me, time_device),
            (side, far, time_device),
            (side, me, (t, sibling_row)),
            (own, far, (t, sibling_row)),
            (side, far, (t, sibling_row)),
        )[which]
        if which == 3:
            src = ext.at[own, far]
        elif which > 3:
            src = ext.at[part, row]
        return pltpu.make_async_remote_copy(
            src_ref=src.at[f],
            dst_ref=ext.at[part, row, f],
            send_sem=halo_send.at[field, which, f],
            recv_sem=halo_recv.at[field, part, row, f],
            device_id=device,
            device_id_type=MESH,
        )

    def sends(field, which):
        return (
            has_far,
            None,
            sends_time(field),
            jnp.logical_and(has_far, sends_time(field)),
            gets_time(field),
            has_far,
            jnp.logical_and(has_far, gets_time(field)),
        )[which]

    def when(cond, act):
        if cond is None:
            act()
        else:
            pl.when(cond)(act)

    def start_halo(field, which, src=None):
        def act():
            for f in range(2):
                halo_copy(field, which, f, src).start()

        when(sends(field, which), act)

    def start_own(field, src):
        for which in (0, 2, 1):
            start_halo(field, which, src)

    def wait_piece(field, part, row, f):
        pltpu.make_async_remote_copy(
            src_ref=exts[field].at[part, row, f],
            dst_ref=exts[field].at[part, row, f],
            send_sem=halo_send.at[field, 0, f],
            recv_sem=halo_recv.at[field, part, row, f],
            device_id=(t, sibling_row),
            device_id_type=MESH,
        ).wait_recv()

    def wait_block(field, part, row, cond=None):
        def act():
            for f in range(2):
                wait_piece(field, part, row, f)

        when(cond, act)

    def forward(field):
        own, side = own_of(field), side_of(field)
        for f in range(2):
            when(has_far, lambda: wait_piece(field, own, far, f))
            when(sends(field, 3), lambda: halo_copy(field, 3, f).start())
        if field < 2:
            start_halo(field, 5)
        for f in range(2):
            when(gets_time(field), lambda: wait_piece(field, side, me, f))
            when(sends(field, 4), lambda: halo_copy(field, 4, f).start())

    def wait_sibling(field):
        wait_block(field, own_of(field), sib)

    def wait_corners(field):
        side = side_of(field)
        wait_block(field, side, far, jnp.logical_and(has_far, gets_time(field)))
        if field < 2:
            start_halo(field, 6)
        wait_block(field, side, sib, gets_time(field))

    def wait_sibling_far(field, corner):
        if corner:
            wait_block(field, side_of(field), sib_far, jnp.logical_and(sib_has_far, gets_time(field)))
        else:
            wait_block(field, own_of(field), sib_far, sib_has_far)

    def finish_sends(field, src):
        for which in range(7 if field < 2 else 5):
            def act(which=which):
                for f in range(2):
                    halo_copy(field, which, f, src).wait_send()

            when(sends(field, which), act)

    start_own(0, video)
    start_own(1, cotangent)

    zeros_block = jnp.zeros((2, C, W), BF16)

    def clear(field, part, row):
        exts[field][part, row] = zeros_block

    for field in range(3):
        own, side = own_of(field), side_of(field)
        no_time = jnp.logical_not(gets_time(field))
        for row, has in ((far, has_far), (sib_far, sib_has_far)):
            none = jnp.logical_not(has)
            when(none, lambda: clear(field, own, row))
            when(jnp.logical_or(no_time, none), lambda: clear(field, side, row))
        for row in (me, sib):
            when(no_time, lambda: clear(field, side, row))

    enters = {
        "me": (me, ((c, 1), (1 - c, 2 * c))),
        "sib": (sib, ((c, 2 - 2 * c), (1 - c, 1))),
        "far": (far, ((c, 2 * c),)),
        "sib_far": (sib_far, ((1 - c, 2 - 2 * c),)),
    }

    def activate(part, name):
        row, targets = enters[name]
        for f in range(2):
            at = 2 * part + f
            value, _ = silu_parts(vext[part, row, f].astype(F32))
            shifted = (lane_shift(value, 1), value, lane_shift(value, -1))
            for q in range(3):
                block = shifted[q].astype(BF16)
                for to in range(2):
                    tt = at - to
                    if 0 <= tt <= 2:
                        for center, p in targets:
                            start = pl.multiple_of((tt * 9 + q) * C + p * 3 * C, 16)
                            stack[center, pl.ds(start, C), to * W : (to + 1) * W] = block

    def turn(src, dst):
        for start in range(0, 5184, W):
            n = min(W, 5184 - start)
            dst[start : start + n, :] = jnp.transpose(src[:, start : start + n])

    def field_pair(ext, tt, p, center):
        at = (2 - tt, 3 - tt)
        return jnp.concatenate([ext[a // 2, center + 1 - p, a % 2] for a in at], axis=1)

    EARLY = [(2, 1), (2, 0), (2, 2), (1, 1), (0, 1)]
    LATE = [(1, 0), (1, 2), (0, 0), (0, 2)]

    def back_terms(ext, k_ref, taps, first):
        for tt, p in taps:
            g = tt * 3 + p
            term = dot(k_ref[g * 576 : (g + 1) * 576, :], field_pair(ext, tt, p, me))
            if first and (tt, p) == taps[0]:
                acc[...] = term
            else:
                acc[...] += term

    def back_sum(f):
        cols = slice(f * W, (f + 1) * W)
        return (
            lane_shift(acc[0:C, cols], -1)
            + acc[C : 2 * C, cols]
            + lane_shift(acc[2 * C : 3 * C, cols], 1)
        )

    zeros64 = jnp.zeros((64, 2 * W), BF16)

    def widened(value, upper):
        lo, hi = value[:W], value[W:C]
        return jnp.concatenate([lo, zeros64, hi] if upper else [lo, hi, zeros64], axis=0)

    def put(layer, m, bx, low, high):
        h, b = m // 2, 3 * (m % 2)
        summed[layer, h, bx, b] = low[:, :W].astype(BF16)
        summed[layer, h, bx, b + 1] = (low[:, W:] + high[:, W:]).astype(BF16)
        summed[layer, h, bx, b + 2] = high[:, :W].astype(BF16)

    def second_chunk(j, upper):
        start, pieces = 16 * ((81 * j) // 8), []
        at = start
        while at < start + CHUNK:
            g = at // 576
            n = min(start + CHUNK, 576 * (g + 1)) - at
            rhs = [widened(field_pair(cext, g // 3, g % 3, center), upper) for center in (1, 2)]
            pieces.append(dot_nt(acts2[at - 576 * g : at - 576 * g + n, :], jnp.concatenate(rhs, axis=1)))
            at += n
        return pieces[0] if len(pieces) == 1 else jnp.concatenate(pieces, axis=0)

    def second_terms(planes):
        for core in range(2):
            @pl.when(c == core)
            def _(core=core):
                for m in planes:
                    for bx in range(2):
                        j = 8 * m + 2 * bx + core
                        put(1, m, bx, second_chunk(j, False), second_chunk(j + 4, True))

    def first_terms(planes):
        rows = [jnp.concatenate([gext[0, center, 0], gext[0, center, 1]], axis=1) for center in (1, 2)]
        rhs = [jnp.concatenate([widened(v, upper) for v in rows], axis=1) for upper in (False, True)]
        for m in planes:
            for bx in range(2):
                out = []
                for upper in range(2):
                    at = pl.ds(chunk_start(8 * m + 4 * upper + 2 * bx + c), CHUNK)
                    out.append(dot_nt(jnp.concatenate([stack[0, at, :], stack[1, at, :]], axis=1), rhs[upper]))
                put(0, m, bx, *out)

    def dev(nxl, ny, nz, nxh):
        return (nxl * 4 + ny, nz * 4 + nxh * 2 + c)

    def remote(src, dst, sems, at, device):
        return pltpu.make_async_remote_copy(
            src_ref=src,
            dst_ref=dst,
            send_sem=sems[0].at[at],
            recv_sem=sems[1].at[at],
            device_id=device,
            device_id_type=MESH,
        )

    def rows_at(start, n):
        return pl.ds(pl.multiple_of(start, 16), n)

    def z_block(nz):
        return nz // 4, 3 * ((nz // 2) % 2) + nz % 2

    def s1_copies(layer, halves=(0, 1)):
        out = []
        for d in (2, 1, 3):
            if 0 in halves:
                ny = lax.rem(y + d, 4)
                src = summed.at[layer, 0, :, :, rows_at(32 * ny, 32), :]
                out.append(
                    remote(src, r1a.at[layer, d - 1], (s1_send, s1_recv), (layer, 0, d - 1), dev(xl, ny, z, xh))
                )
            if 1 in halves:
                nx = lax.rem(x + d, 4)
                src = summed.at[layer, 1, nx // 2, :, rows_at(64 * (nx % 2), 64), :]
                out.append(
                    remote(src, r1b.at[layer, d - 1], (s1_send, s1_recv), (layer, 1, d - 1), dev(nx % 2, y, z, nx // 2))
                )
        return out

    def s2_copies(layer):
        out = []
        for d in (2, 1, 3):
            ny, nx = lax.rem(y + d, 4), lax.rem(x + d, 4)
            src = ta.at[layer, nx // 2, :, rows_at(16 * (nx % 2), 16), :]
            out.append(
                remote(src, r2a.at[layer, d - 1], (s2_send, s2_recv), (layer, 0, d - 1), dev(nx % 2, y, z, nx // 2))
            )
            src = tb.at[layer, :, rows_at(16 * ny, 16), :]
            out.append(remote(src, r2b.at[layer, d - 1], (s2_send, s2_recv), (layer, 1, d - 1), dev(xl, ny, z, xh)))
        return out

    def s3_copies(layer):
        out = []
        for d in (4, 3, 5, 2, 6, 1, 7):
            nz = lax.rem(z + d, 8)
            nh, nb = z_block(nz)
            src = ub.at[layer, nh, pl.ds(nb, 2)]
            out.append(remote(src, r3.at[layer, d - 1], (s3_send, s3_recv), (layer, d - 1), dev(xl, y, nz, xh)))
        return out

    def z_off(steps):
        return lax.rem(z + steps * (1 - 2 * c) + 8, 8)

    def z_part(layer, nz):
        nh, nb = z_block(nz)
        return summed.at[layer, nh, :, pl.ds(nb, 2), 128:CHUNK, :]

    relays = ((4, 1), (2, 1), (-3, -1))

    def z1_copies(layer):
        out = []
        for k, (to, hop) in enumerate(relays):
            src = z_part(layer, z_off(to))
            out.append(remote(src, rz1.at[layer, k], (z1_send, z1_recv), (layer, k), dev(xl, y, z_off(hop), xh)))
        return out

    def z2_copies(layer):
        out = []
        for k, (to, hop) in enumerate(relays):
            device = dev(xl, y, z_off(to - hop), xh)
            out.append(remote(tz.at[layer, k], rz2.at[layer, k], (z2_send, z2_recv), (layer, k), device))
        src = z_part(layer, z_off(-1))
        out.append(remote(src, rz2.at[layer, 3], (z2_send, z2_recv), (layer, 3), dev(xl, y, z_off(-1), xh)))
        return out

    upper = z % 2
    place = 4 * x + y

    def plane_src(layer, nx, ny):
        return tc.at[layer, nx // 2, lax.rem(upper + nx, 2), rows_at(16 * jnp.minimum(ny, 2), 16), :]

    def plane_copies(layer):
        out = []
        for e in (10, 9, 11, 6, 14, 8, 2, 5, 7, 13, 15, 4, 12, 1, 3):
            to = lax.rem(place + e, 16)
            nx, ny = to // 4, to % 4
            src = plane_src(layer, nx, ny)
            device = dev(nx % 2, ny, z, nx // 2)
            out.append(remote(src, rp.at[layer, e - 1], (p_send, p_recv), (layer, e - 1), device))
        return out

    def s4_copies(layer):
        out = []
        for e in range(1, 8):
            device = (lax.rem(t + e, 8), r)
            out.append(remote(r4.at[layer, 0], r4.at[layer, e], (s4_send, s4_recv), (layer, e - 1), device))
        return out

    def wide(value):
        return value.astype(F32)

    def start_all(copies):
        for copy in copies:
            copy.start()

    def wait_all(copies):
        for copy in copies:
            copy.wait()

    def relay(layer):
        wait_all(z1_copies(layer))
        for k, (to, hop) in enumerate(relays):
            own = z_part(layer, z_off(to - hop))[...]
            tz[layer, k] = (wide(own) + wide(rz1[layer, k])).astype(BF16)
        start_all(z2_copies(layer))

    def plane(layer):
        wait_all(z2_copies(layer))
        total = wide(z_part(layer, z)[...])
        for k in range(4):
            total += wide(rz2[layer, k])
        tc[layer] = total.astype(BF16)
        start_all(plane_copies(layer))

    def stage2(layer):
        wait_all(s1_copies(layer))
        own = summed[layer, 0, :, :, rows_at(32 * y, 32), :]
        ta[layer] = (wide(own) + wide(r1a[layer, 0]) + wide(r1a[layer, 1]) + wide(r1a[layer, 2])).astype(BF16)
        own = summed[layer, 1, xh, :, rows_at(64 * xl, 64), :]
        tb[layer] = (wide(own) + wide(r1b[layer, 0]) + wide(r1b[layer, 1]) + wide(r1b[layer, 2])).astype(BF16)
        start_all(s2_copies(layer))

    def stage3(layer):
        wait_all(s2_copies(layer))
        own = ta[layer, xh, :, rows_at(16 * xl, 16), :]
        ub[layer, 0] = (wide(own) + wide(r2a[layer, 0]) + wide(r2a[layer, 1]) + wide(r2a[layer, 2])).astype(BF16)
        own = tb[layer, :, rows_at(16 * y, 16), :]
        ub[layer, 1] = (wide(own) + wide(r2b[layer, 0]) + wide(r2b[layer, 1]) + wide(r2b[layer, 2])).astype(BF16)
        start_all(s3_copies(layer))

    my_half, my_block = z_block(z)
    scale = 1.0 / math.sqrt(TM * 2 * ROWS * W)

    def stage4(layer):
        wait_all(plane_copies(layer))
        total = wide(plane_src(layer, x, y)[...])
        for e in range(15):
            total += wide(rp[layer, e])
        r4[layer, 0, 2] = total.astype(BF16)
        wait_all(s3_copies(layer))
        for k in range(2):
            total = wide(ub[layer, my_half, my_block + k])
            for d in range(7):
                total += wide(r3[layer, d, k])
            r4[layer, 0, k] = total.astype(BF16)
        start_all(s4_copies(layer))

    def unpacked(value):
        return jnp.where(upper == 0, value, pltpu.roll(value, 64, 1))

    def stage5(layer):
        wait_all(s4_copies(layer))
        for e in range(8):
            u = lax.rem(t + 8 - e, 8)
            uy, ux = u % 4, u // 4
            start = jnp.where(my_half == 0, 32 * uy + 16 * ux, 64 * ux + 16 * uy)
            final[rows_at(start, 16), :W] = wide(r4[layer, e, upper]) * scale
            final[rows_at(start, 16), W:] = unpacked(wide(r4[layer, e, 1 - upper]) * scale)
            start = 128 + 16 * jnp.minimum(uy, 2)
            value = wide(r4[layer, e, 2]) * scale

            @pl.when(jnp.logical_and(ux == 0, uy < 3))
            def _(start=start, value=value):
                final[rows_at(start, 16), :W] = value

            @pl.when(jnp.logical_and(ux == 1, uy < 3))
            def _(start=start, value=value):
                final[rows_at(start, 16), W:] = unpacked(value)

        off = 4 * (z % 2) + 2 * xh + c
        for k in range(8):
            @pl.when(off == k)
            def _(k=k):
                k_grad[layer] = final[2 * k : 2 * k + 162, :C]

    loads[0].wait()
    activate(1, "me")
    loads[3].wait()
    turn(k2t, k2)
    loads[2].wait()
    turn(k1t, k1)
    forward(0)
    activate(0, "me")
    activate(1, "far")
    wait_sibling(0)
    activate(1, "sib")
    late = dot(k1t[:, 3456:], stack[c, 3456:, :])
    forward(1)
    loads[1].wait()
    wait_sibling(1)
    back_terms(cext, k2, EARLY, True)
    wait_corners(0)
    activate(0, "far")
    activate(0, "sib")
    out = late + dot(k1t[:, :3456], stack[c, :3456, :])
    for f in range(2):
        value = out[:, f * W : (f + 1) * W].astype(BF16)
        x1[f] = value
        value, _ = silu_parts(value.astype(F32))
        a2[c, f] = value.astype(BF16)
    a2_copy = pltpu.make_async_remote_copy(
        src_ref=a2.at[c],
        dst_ref=a2.at[c],
        send_sem=a2_sem.at[0],
        recv_sem=a2_sem.at[1],
        device_id=(t, sibling_row),
        device_id_type=MESH,
    )
    a2_copy.start()
    wait_sibling_far(0, False)
    activate(1, "sib_far")
    wait_sibling_far(1, False)
    a2_copy.wait_recv()
    for center in range(2):
        for f in range(2):
            value = a2[center, f].astype(F32)
            shifted = (lane_shift(value, 1), value, lane_shift(value, -1))
            cols = slice((2 * center + f) * W, (2 * center + f + 1) * W)
            for q in range(3):
                acts2[q * C : (q + 1) * C, cols] = shifted[q].astype(BF16)
    second_terms([3])
    wait_corners(1)
    back_terms(cext, k2, LATE, False)
    for f in range(2):
        _, slope = silu_parts(x1[f].astype(F32))
        gext[0, me, f] = (back_sum(f) * slope).astype(BF16)
    start_halo(2, 1, gext.at[0, me])
    wait_sibling_far(1, True)
    second_terms([2])
    start_all(s1_copies(1, (1,)))
    second_terms([0, 1])
    start_all(s1_copies(1, (0,)))
    start_all(z1_copies(1))

    wait_sibling_far(0, True)
    activate(0, "sib_far")
    wait_sibling(2)
    first_terms((2, 3))
    start_all(s1_copies(0, (1,)))
    first_terms((0, 1))
    start_all(s1_copies(0, (0,)))
    start_all(z1_copies(0))
    relay(1)
    stage2(1)
    relay(0)
    stage2(0)
    start_halo(2, 0, gext.at[0, me])
    start_halo(2, 2, gext.at[0, me])
    plane(1)
    stage3(1)
    plane(0)
    stage3(0)
    forward(2)
    back_terms(gext, k1, EARLY, True)
    stage4(1)
    stage4(0)
    wait_corners(2)
    back_terms(gext, k1, LATE, False)
    for f in range(2):
        _, slope = silu_parts(vext[1, me, f].astype(F32))
        in_grad[f, 0] = (back_sum(f) * slope).astype(BF16)

    stage5(1)
    stage5(0)
    finish_sends(0, video)
    finish_sends(1, cotangent)
    finish_sends(2, gext.at[0, me])
    a2_copy.wait_send()


def finish(in_src, k_src, in_dst, k_dst):
    in_dst[:, 0] = in_src[:, 0]
    for layer in range(2):
        k_dst[:, layer, :] = k_src[layer]


def on_device(video_in, kernels, cotangent):
    dma = pltpu.SemaphoreType.DMA
    any_spec = pl.BlockSpec(memory_space=pl.ANY)
    vmem_spec = pl.BlockSpec(memory_space=pltpu.VMEM)
    in_grad, k_grad = pl.pallas_call(
        kernel,
        out_shape=(
            jax.ShapeDtypeStruct((2, 1, C, W), BF16),
            jax.ShapeDtypeStruct((2, 162, C), F32),
        ),
        in_specs=[any_spec] * 3,
        out_specs=(vmem_spec, vmem_spec),
        scratch_shapes=[
            pltpu.VMEM((C, 5184), BF16),
            pltpu.VMEM((C, 5184), BF16),
            pltpu.VMEM((5184, C), BF16),
            pltpu.VMEM((5184, C), BF16),
            pltpu.VMEM((2, 4, 2, C, W), BF16),
            pltpu.VMEM((2, 4, 2, C, W), BF16),
            pltpu.VMEM((2, 4, 2, C, W), BF16),
            pltpu.VMEM((2, 5184, 2 * W), BF16),
            pltpu.VMEM((2, 2, C, W), BF16),
            pltpu.VMEM((3 * C, 4 * W), BF16),
            pltpu.VMEM((3 * C, 2 * W), F32),
            pltpu.VMEM((2, C, W), BF16),
            pltpu.VMEM((2, 2, 2, 6, CHUNK, W), BF16),
            pltpu.VMEM((2, 3, 2, 6, 32, W), BF16),
            pltpu.VMEM((2, 3, 6, 64, W), BF16),
            pltpu.VMEM((2, 2, 6, 32, W), BF16),
            pltpu.VMEM((2, 6, 64, W), BF16),
            pltpu.VMEM((2, 3, 6, 16, W), BF16),
            pltpu.VMEM((2, 3, 6, 16, W), BF16),
            pltpu.VMEM((2, 2, 6, 16, W), BF16),
            pltpu.VMEM((2, 7, 2, 16, W), BF16),
            pltpu.VMEM((2, 3, 2, 2, 48, W), BF16),
            pltpu.VMEM((2, 3, 2, 2, 48, W), BF16),
            pltpu.VMEM((2, 4, 2, 2, 48, W), BF16),
            pltpu.VMEM((2, 2, 2, 48, W), BF16),
            pltpu.VMEM((2, 15, 16, W), BF16),
            pltpu.VMEM((2, 8, 3, 16, W), BF16),
            pltpu.VMEM((CHUNK, 2 * W), F32),
            dma((4,)),
            dma((3, 7, 2)),
            dma((3, 2, 4, 2)),
            dma((2,)),
            dma((2, 2, 3)),
            dma((2, 2, 3)),
            dma((2, 2, 3)),
            dma((2, 2, 3)),
            dma((2, 7)),
            dma((2, 7)),
            dma((2, 3)),
            dma((2, 3)),
            dma((2, 4)),
            dma((2, 4)),
            dma((2, 15)),
            dma((2, 15)),
            dma((2, 7)),
            dma((2, 7)),
        ],
        compiler_params=pltpu.CompilerParams(
            collective_id=0, has_side_effects=True, vmem_limit_bytes=56 * 2**20
        ),
        cost_estimate=pl.CostEstimate(flops=2600000000, bytes_accessed=6000000, transcendentals=500000),
    )(video_in.reshape(2, C, W), jnp.swapaxes(kernels, 1, 2), cotangent.reshape(2, C, W))
    in_grad, k_grad = pl.pallas_call(
        finish,
        out_shape=(
            jax.ShapeDtypeStruct((2, 1, C, W), BF16),
            jax.ShapeDtypeStruct((162, 2, C), F32),
        ),
        in_specs=[vmem_spec, vmem_spec],
        out_specs=(vmem_spec, vmem_spec),
    )(in_grad, k_grad)
    return in_grad, jnp.swapaxes(k_grad, 0, 1)


def solution(mesh):
    return jax.shard_map(
        on_device,
        mesh=mesh,
        in_specs=(P("tm", "rows", None, None), P(), P("tm", "rows", None, None)),
        out_specs=(P("tm", "rows", None, None), P(None, "rows", None)),
        check_vma=False,
    )
```

```python
import math

import jax
import jax.numpy as jnp
from jax import lax
from jax.experimental import pallas as pl
from jax.experimental.pallas import tpu as pltpu
from jax.sharding import PartitionSpec as P

MESH = pl.DeviceIdType.MESH
F32 = jnp.float32
BF16 = jnp.bfloat16
C = 192
W = 128
TM = 8
ROWS = 32
CHUNK = 176


def dot(a, b):
    return lax.dot_general(a, b, (((1,), (0,)), ((), ())), preferred_element_type=F32)


def dot_nt(a, b):
    return lax.dot_general(a, b, (((1,), (1,)), ((), ())), preferred_element_type=F32)


def lane_shift(value, by):
    rolled = pltpu.roll(value, by % W, 1)
    col = lax.broadcasted_iota(jnp.int32, value.shape, 1)
    edge = 0 if by == 1 else W - 1
    return jnp.where(col == edge, 0.0, rolled)


def silu_parts(value):
    sigma = jax.nn.sigmoid(value)
    return value * sigma, sigma * (1.0 + value * (1.0 - sigma))


def chunk_start(j):
    return pl.multiple_of(16 * ((81 * j) // 8), 16)


def kernel(
    video, kernels, cotangent, in_grad, k_grad,
    k1t, k2t, k1, k2, vext, cext, gext, stack, a2, acts2, acc, x1, summed,
    r1a, r1b, ta, tb, r2a, r2b, ub, r3, rz1, tz, rz2, tc, rp, r4,
    load_sem, halo_send, halo_recv, a2_sem,
    s1_send, s1_recv, s2_send, s2_recv, s3_send, s3_recv, z1_send, z1_recv, z2_send, z2_recv,
    p_send, p_recv, s4_send, s4_recv,
):
    t = lax.axis_index("tm")
    r = lax.axis_index("rows")
    xl, y = t // 4, t % 4
    z, xh, c = r // 4, (r // 2) % 2, r % 2
    x = 2 * xh + xl
    has_far = jnp.logical_and(r > 0, r < ROWS - 1)
    far_row, sibling_row = r - 1 + 2 * c, r + 1 - 2 * c
    me, sib, far, sib_far = 1 + c, 2 - c, 3 * c, 3 - 3 * c
    sib_has_far = jnp.logical_and(sibling_row > 0, sibling_row < ROWS - 1)
    has_past, has_future = t > 0, t < TM - 1

    loads = [
        pltpu.make_async_copy(video, vext.at[1, me], load_sem.at[0]),
        pltpu.make_async_copy(cotangent, cext.at[0, me], load_sem.at[1]),
        pltpu.make_async_copy(kernels.at[0], k1t, load_sem.at[2]),
        pltpu.make_async_copy(kernels.at[1], k2t, load_sem.at[3]),
    ]
    for load in loads:
        load.start()

    barrier = pltpu.get_barrier_semaphore()

    def greet(device):
        pl.semaphore_signal(barrier, inc=1, device_id=device, device_id_type=MESH)

    for e in range(1, 8):
        greet((lax.rem(t + e, 8), r))
        greet((t, lax.rem(z + e, 8) * 4 + xh * 2 + c))
    for e in range(8):
        greet((lax.rem(t + e, 8), z * 4 + (1 - xh) * 2 + c))
    greet((t, sibling_row))

    @pl.when(has_far)
    def _():
        greet((t, far_row))

    pl.semaphore_wait(barrier, 23 + jnp.where(has_far, 1, 0))

    exts = (vext, cext, gext)

    def own_of(field):
        return 1 if field == 0 else 0

    def side_of(field):
        return 0 if field == 0 else 1

    def sends_time(field):
        return has_future if field == 0 else has_past

    def gets_time(field):
        return has_past if field == 0 else has_future

    def halo_copy(field, which, f, src=None):
        own, side, ext = own_of(field), side_of(field), exts[field]
        time_device = (t + 1, r) if field == 0 else (t - 1, r)
        part, row, device = (
            (own, sib_far, (t, far_row)),
            (own, me, (t, sibling_row)),
            (side, me, time_device),
            (side, far, time_device),
            (side, me, (t, sibling_row)),
            (own, far, (t, sibling_row)),
            (side, far, (t, sibling_row)),
        )[which]
        if which == 3:
            src = ext.at[own, far]
        elif which > 3:
            src = ext.at[part, row]
        return pltpu.make_async_remote_copy(
            src_ref=src.at[f],
            dst_ref=ext.at[part, row, f],
            send_sem=halo_send.at[field, which, f],
            recv_sem=halo_recv.at[field, part, row, f],
            device_id=device,
            device_id_type=MESH,
        )

    def sends(field, which):
        return (
            has_far,
            None,
            sends_time(field),
            jnp.logical_and(has_far, sends_time(field)),
            gets_time(field),
            has_far,
            jnp.logical_and(has_far, gets_time(field)),
        )[which]

    def when(cond, act):
        if cond is None:
            act()
        else:
            pl.when(cond)(act)

    def start_halo(field, which, src=None):
        def act():
            for f in range(2):
                halo_copy(field, which, f, src).start()

        when(sends(field, which), act)

    def start_own(field, src):
        for which in (0, 2, 1):
            start_halo(field, which, src)

    def wait_piece(field, part, row, f):
        pltpu.make_async_remote_copy(
            src_ref=exts[field].at[part, row, f],
            dst_ref=exts[field].at[part, row, f],
            send_sem=halo_send.at[field, 0, f],
            recv_sem=halo_recv.at[field, part, row, f],
            device_id=(t, sibling_row),
            device_id_type=MESH,
        ).wait_recv()

    def wait_block(field, part, row, cond=None):
        def act():
            for f in range(2):
                wait_piece(field, part, row, f)

        when(cond, act)

    def forward(field):
        own, side = own_of(field), side_of(field)
        for f in range(2):
            when(has_far, lambda: wait_piece(field, own, far, f))
            when(sends(field, 3), lambda: halo_copy(field, 3, f).start())
        if field < 2:
            start_halo(field, 5)
        for f in range(2):
            when(gets_time(field), lambda: wait_piece(field, side, me, f))
            when(sends(field, 4), lambda: halo_copy(field, 4, f).start())

    def wait_sibling(field):
        wait_block(field, own_of(field), sib)

    def wait_corners(field):
        side = side_of(field)
        wait_block(field, side, far, jnp.logical_and(has_far, gets_time(field)))
        if field < 2:
            start_halo(field, 6)
        wait_block(field, side, sib, gets_time(field))

    def wait_sibling_far(field, corner):
        if corner:
            wait_block(field, side_of(field), sib_far, jnp.logical_and(sib_has_far, gets_time(field)))
        else:
            wait_block(field, own_of(field), sib_far, sib_has_far)

    def finish_sends(field, src):
        for which in range(7 if field < 2 else 5):
            def act(which=which):
                for f in range(2):
                    halo_copy(field, which, f, src).wait_send()

            when(sends(field, which), act)

    start_own(0, video)
    start_own(1, cotangent)

    zeros_block = jnp.zeros((2, C, W), BF16)

    def clear(field, part, row):
        exts[field][part, row] = zeros_block

    for field in range(3):
        own, side = own_of(field), side_of(field)
        no_time = jnp.logical_not(gets_time(field))
        for row, has in ((far, has_far), (sib_far, sib_has_far)):
            none = jnp.logical_not(has)
            when(none, lambda: clear(field, own, row))
            when(jnp.logical_or(no_time, none), lambda: clear(field, side, row))
        for row in (me, sib):
            when(no_time, lambda: clear(field, side, row))

    enters = {
        "me": (me, ((c, 1), (1 - c, 2 * c))),
        "sib": (sib, ((c, 2 - 2 * c), (1 - c, 1))),
        "far": (far, ((c, 2 * c),)),
        "sib_far": (sib_far, ((1 - c, 2 - 2 * c),)),
    }

    def activate(part, name):
        row, targets = enters[name]
        for f in range(2):
            at = 2 * part + f
            value, _ = silu_parts(vext[part, row, f].astype(F32))
            shifted = (lane_shift(value, 1), value, lane_shift(value, -1))
            for q in range(3):
                block = shifted[q].astype(BF16)
                for to in range(2):
                    tt = at - to
                    if 0 <= tt <= 2:
                        for center, p in targets:
                            start = pl.multiple_of((tt * 9 + q) * C + p * 3 * C, 16)
                            stack[center, pl.ds(start, C), to * W : (to + 1) * W] = block

    def turn(src, dst):
        for start in range(0, 5184, W):
            n = min(W, 5184 - start)
            dst[start : start + n, :] = jnp.transpose(src[:, start : start + n])

    def field_pair(ext, tt, p, center):
        at = (2 - tt, 3 - tt)
        return jnp.concatenate([ext[a // 2, center + 1 - p, a % 2] for a in at], axis=1)

    EARLY = [(2, 1), (2, 0), (2, 2), (1, 1), (0, 1)]
    LATE = [(1, 0), (1, 2), (0, 0), (0, 2)]

    def back_terms(ext, k_ref, taps, first):
        for tt, p in taps:
            g = tt * 3 + p
            term = dot(k_ref[g * 576 : (g + 1) * 576, :], field_pair(ext, tt, p, me))
            if first and (tt, p) == taps[0]:
                acc[...] = term
            else:
                acc[...] += term

    def back_sum(f):
        cols = slice(f * W, (f + 1) * W)
        return (
            lane_shift(acc[0:C, cols], -1)
            + acc[C : 2 * C, cols]
            + lane_shift(acc[2 * C : 3 * C, cols], 1)
        )

    zeros64 = jnp.zeros((64, 2 * W), BF16)

    def widened(value, upper):
        lo, hi = value[:W], value[W:C]
        return jnp.concatenate([lo, zeros64, hi] if upper else [lo, hi, zeros64], axis=0)

    def put(layer, m, bx, low, high):
        h, b = m // 2, 3 * (m % 2)
        summed[layer, h, bx, b] = low[:, :W].astype(BF16)
        summed[layer, h, bx, b + 1] = (low[:, W:] + high[:, W:]).astype(BF16)
        summed[layer, h, bx, b + 2] = high[:, :W].astype(BF16)

    def second_chunk(j, upper):
        start, pieces = 16 * ((81 * j) // 8), []
        at = start
        while at < start + CHUNK:
            g = at // 576
            n = min(start + CHUNK, 576 * (g + 1)) - at
            rhs = [widened(field_pair(cext, g // 3, g % 3, center), upper) for center in (1, 2)]
            pieces.append(dot_nt(acts2[at - 576 * g : at - 576 * g + n, :], jnp.concatenate(rhs, axis=1)))
            at += n
        return pieces[0] if len(pieces) == 1 else jnp.concatenate(pieces, axis=0)

    def second_terms(planes):
        for core in range(2):
            @pl.when(c == core)
            def _(core=core):
                for m in planes:
                    for bx in range(2):
                        j = 8 * m + 2 * bx + core
                        put(1, m, bx, second_chunk(j, False), second_chunk(j + 4, True))

    def first_terms(planes):
        rows = [jnp.concatenate([gext[0, center, 0], gext[0, center, 1]], axis=1) for center in (1, 2)]
        rhs = [jnp.concatenate([widened(v, upper) for v in rows], axis=1) for upper in (False, True)]
        for m in planes:
            for bx in range(2):
                out = []
                for upper in range(2):
                    at = pl.ds(chunk_start(8 * m + 4 * upper + 2 * bx + c), CHUNK)
                    out.append(dot_nt(jnp.concatenate([stack[0, at, :], stack[1, at, :]], axis=1), rhs[upper]))
                put(0, m, bx, *out)

    def dev(nxl, ny, nz, nxh):
        return (nxl * 4 + ny, nz * 4 + nxh * 2 + c)

    def remote(src, dst, sems, at, device):
        return pltpu.make_async_remote_copy(
            src_ref=src,
            dst_ref=dst,
            send_sem=sems[0].at[at],
            recv_sem=sems[1].at[at],
            device_id=device,
            device_id_type=MESH,
        )

    def rows_at(start, n):
        return pl.ds(pl.multiple_of(start, 16), n)

    def z_block(nz):
        return nz // 4, 3 * ((nz // 2) % 2) + nz % 2

    def s1_copies(layer, halves=(0, 1)):
        out = []
        for d in (2, 1, 3):
            if 0 in halves:
                ny = lax.rem(y + d, 4)
                src = summed.at[layer, 0, :, :, rows_at(32 * ny, 32), :]
                out.append(
                    remote(src, r1a.at[layer, d - 1], (s1_send, s1_recv), (layer, 0, d - 1), dev(xl, ny, z, xh))
                )
            if 1 in halves:
                nx = lax.rem(x + d, 4)
                src = summed.at[layer, 1, nx // 2, :, rows_at(64 * (nx % 2), 64), :]
                out.append(
                    remote(src, r1b.at[layer, d - 1], (s1_send, s1_recv), (layer, 1, d - 1), dev(nx % 2, y, z, nx // 2))
                )
        return out

    def s2_copies(layer):
        out = []
        for d in (2, 1, 3):
            ny, nx = lax.rem(y + d, 4), lax.rem(x + d, 4)
            src = ta.at[layer, nx // 2, :, rows_at(16 * (nx % 2), 16), :]
            out.append(
                remote(src, r2a.at[layer, d - 1], (s2_send, s2_recv), (layer, 0, d - 1), dev(nx % 2, y, z, nx // 2))
            )
            src = tb.at[layer, :, rows_at(16 * ny, 16), :]
            out.append(remote(src, r2b.at[layer, d - 1], (s2_send, s2_recv), (layer, 1, d - 1), dev(xl, ny, z, xh)))
        return out

    def s3_copies(layer):
        out = []
        for d in (4, 3, 5, 2, 6, 1, 7):
            nz = lax.rem(z + d, 8)
            nh, nb = z_block(nz)
            src = ub.at[layer, nh, pl.ds(nb, 2)]
            out.append(remote(src, r3.at[layer, d - 1], (s3_send, s3_recv), (layer, d - 1), dev(xl, y, nz, xh)))
        return out

    def z_off(steps):
        return lax.rem(z + steps * (1 - 2 * c) + 8, 8)

    def z_part(layer, nz):
        nh, nb = z_block(nz)
        return summed.at[layer, nh, :, pl.ds(nb, 2), 128:CHUNK, :]

    relays = ((4, 1), (2, 1), (-3, -1))

    def z1_copies(layer):
        out = []
        for k, (to, hop) in enumerate(relays):
            src = z_part(layer, z_off(to))
            out.append(remote(src, rz1.at[layer, k], (z1_send, z1_recv), (layer, k), dev(xl, y, z_off(hop), xh)))
        return out

    def z2_copies(layer):
        out = []
        for k, (to, hop) in enumerate(relays):
            device = dev(xl, y, z_off(to - hop), xh)
            out.append(remote(tz.at[layer, k], rz2.at[layer, k], (z2_send, z2_recv), (layer, k), device))
        src = z_part(layer, z_off(-1))
        out.append(remote(src, rz2.at[layer, 3], (z2_send, z2_recv), (layer, 3), dev(xl, y, z_off(-1), xh)))
        return out

    upper = z % 2
    place = 4 * x + y

    def plane_src(layer, nx, ny):
        return tc.at[layer, nx // 2, lax.rem(upper + nx, 2), rows_at(16 * jnp.minimum(ny, 2), 16), :]

    def plane_copies(layer):
        out = []
        for e in (10, 9, 11, 6, 14, 8, 2, 5, 7, 13, 15, 4, 12, 1, 3):
            to = lax.rem(place + e, 16)
            nx, ny = to // 4, to % 4
            src = plane_src(layer, nx, ny)
            device = dev(nx % 2, ny, z, nx // 2)
            out.append(remote(src, rp.at[layer, e - 1], (p_send, p_recv), (layer, e - 1), device))
        return out

    def s4_copies(layer):
        out = []
        for e in range(1, 8):
            device = (lax.rem(t + e, 8), r)
            out.append(remote(r4.at[layer, 0], r4.at[layer, e], (s4_send, s4_recv), (layer, e - 1), device))
        return out

    def wide(value):
        return value.astype(F32)

    def start_all(copies):
        for copy in copies:
            copy.start()

    def wait_all(copies):
        for copy in copies:
            copy.wait()

    def relay(layer):
        wait_all(z1_copies(layer))
        for k, (to, hop) in enumerate(relays):
            own = z_part(layer, z_off(to - hop))[...]
            tz[layer, k] = (wide(own) + wide(rz1[layer, k])).astype(BF16)
        start_all(z2_copies(layer))

    def plane(layer):
        wait_all(z2_copies(layer))
        total = wide(z_part(layer, z)[...])
        for k in range(4):
            total += wide(rz2[layer, k])
        tc[layer] = total.astype(BF16)
        start_all(plane_copies(layer))

    def stage2(layer):
        wait_all(s1_copies(layer))
        own = summed[layer, 0, :, :, rows_at(32 * y, 32), :]
        ta[layer] = (wide(own) + wide(r1a[layer, 0]) + wide(r1a[layer, 1]) + wide(r1a[layer, 2])).astype(BF16)
        own = summed[layer, 1, xh, :, rows_at(64 * xl, 64), :]
        tb[layer] = (wide(own) + wide(r1b[layer, 0]) + wide(r1b[layer, 1]) + wide(r1b[layer, 2])).astype(BF16)
        start_all(s2_copies(layer))

    def stage3(layer):
        wait_all(s2_copies(layer))
        own = ta[layer, xh, :, rows_at(16 * xl, 16), :]
        ub[layer, 0] = (wide(own) + wide(r2a[layer, 0]) + wide(r2a[layer, 1]) + wide(r2a[layer, 2])).astype(BF16)
        own = tb[layer, :, rows_at(16 * y, 16), :]
        ub[layer, 1] = (wide(own) + wide(r2b[layer, 0]) + wide(r2b[layer, 1]) + wide(r2b[layer, 2])).astype(BF16)
        start_all(s3_copies(layer))

    my_half, my_block = z_block(z)
    scale = 1.0 / math.sqrt(TM * 2 * ROWS * W)

    def stage4(layer):
        wait_all(plane_copies(layer))
        total = wide(plane_src(layer, x, y)[...])
        for e in range(15):
            total += wide(rp[layer, e])
        r4[layer, 0, 2] = total.astype(BF16)
        wait_all(s3_copies(layer))
        for k in range(2):
            total = wide(ub[layer, my_half, my_block + k])
            for d in range(7):
                total += wide(r3[layer, d, k])
            r4[layer, 0, k] = total.astype(BF16)
        start_all(s4_copies(layer))

    def unpacked(value):
        return jnp.where(upper == 0, value, pltpu.roll(value, 64, 1))

    def stage5(layer):
        wait_all(s4_copies(layer))
        for e in range(8):
            u = lax.rem(t + 8 - e, 8)
            uy, ux = u % 4, u // 4
            start = jnp.where(my_half == 0, 32 * uy + 16 * ux, 64 * ux + 16 * uy)
            k_grad[layer, rows_at(start, 16), :W] = wide(r4[layer, e, upper]) * scale
            k_grad[layer, rows_at(start, 16), W:] = unpacked(wide(r4[layer, e, 1 - upper]) * scale)
            start = 128 + 16 * jnp.minimum(uy, 2)
            value = wide(r4[layer, e, 2]) * scale

            @pl.when(jnp.logical_and(ux == 0, uy < 3))
            def _(start=start, value=value):
                k_grad[layer, rows_at(start, 16), :W] = value

            @pl.when(jnp.logical_and(ux == 1, uy < 3))
            def _(start=start, value=value):
                k_grad[layer, rows_at(start, 16), W:] = unpacked(value)

    loads[0].wait()
    activate(1, "me")
    loads[3].wait()
    turn(k2t, k2)
    loads[2].wait()
    turn(k1t, k1)
    forward(0)
    activate(0, "me")
    activate(1, "far")
    wait_sibling(0)
    activate(1, "sib")
    late = dot(k1t[:, 3456:], stack[c, 3456:, :])
    forward(1)
    loads[1].wait()
    wait_sibling(1)
    back_terms(cext, k2, EARLY, True)
    wait_corners(0)
    activate(0, "far")
    activate(0, "sib")
    out = late + dot(k1t[:, :3456], stack[c, :3456, :])
    for f in range(2):
        value = out[:, f * W : (f + 1) * W].astype(BF16)
        x1[f] = value
        value, _ = silu_parts(value.astype(F32))
        a2[c, f] = value.astype(BF16)
    a2_copy = pltpu.make_async_remote_copy(
        src_ref=a2.at[c],
        dst_ref=a2.at[c],
        send_sem=a2_sem.at[0],
        recv_sem=a2_sem.at[1],
        device_id=(t, sibling_row),
        device_id_type=MESH,
    )
    a2_copy.start()
    wait_sibling_far(0, False)
    activate(1, "sib_far")
    wait_sibling_far(1, False)
    a2_copy.wait_recv()
    for center in range(2):
        for f in range(2):
            value = a2[center, f].astype(F32)
            shifted = (lane_shift(value, 1), value, lane_shift(value, -1))
            cols = slice((2 * center + f) * W, (2 * center + f + 1) * W)
            for q in range(3):
                acts2[q * C : (q + 1) * C, cols] = shifted[q].astype(BF16)
    second_terms([3])
    wait_corners(1)
    back_terms(cext, k2, LATE, False)
    for f in range(2):
        _, slope = silu_parts(x1[f].astype(F32))
        gext[0, me, f] = (back_sum(f) * slope).astype(BF16)
    start_halo(2, 1, gext.at[0, me])
    wait_sibling_far(1, True)
    second_terms([2])
    start_all(s1_copies(1, (1,)))
    second_terms([0, 1])
    start_all(s1_copies(1, (0,)))
    start_all(z1_copies(1))

    wait_sibling_far(0, True)
    activate(0, "sib_far")
    wait_sibling(2)
    first_terms((2, 3))
    start_all(s1_copies(0, (1,)))
    first_terms((0, 1))
    start_all(s1_copies(0, (0,)))
    start_all(z1_copies(0))
    relay(1)
    stage2(1)
    relay(0)
    stage2(0)
    start_halo(2, 0, gext.at[0, me])
    start_halo(2, 2, gext.at[0, me])
    plane(1)
    stage3(1)
    plane(0)
    stage3(0)
    forward(2)
    back_terms(gext, k1, EARLY, True)
    stage4(1)
    stage4(0)
    wait_corners(2)
    back_terms(gext, k1, LATE, False)
    for f in range(2):
        _, slope = silu_parts(vext[1, me, f].astype(F32))
        in_grad[f, 0] = (back_sum(f) * slope).astype(BF16)

    stage5(1)
    stage5(0)
    finish_sends(0, video)
    finish_sends(1, cotangent)
    finish_sends(2, gext.at[0, me])
    a2_copy.wait_send()


def finish(in_src, k_src, in_dst, k_dst):
    in_dst[:, 0] = in_src[:, 0]
    off = lax.axis_index("rows") % 8
    for k in range(8):
        @pl.when(off == k)
        def _(k=k):
            for layer in range(2):
                k_dst[:, layer, :] = k_src[layer, 2 * k : 2 * k + 162, :C]


def on_device(video_in, kernels, cotangent):
    dma = pltpu.SemaphoreType.DMA
    any_spec = pl.BlockSpec(memory_space=pl.ANY)
    vmem_spec = pl.BlockSpec(memory_space=pltpu.VMEM)
    in_grad, k_grad = pl.pallas_call(
        kernel,
        out_shape=(
            jax.ShapeDtypeStruct((2, 1, C, W), BF16),
            jax.ShapeDtypeStruct((2, CHUNK, 2 * W), F32),
        ),
        in_specs=[any_spec] * 3,
        out_specs=(vmem_spec, vmem_spec),
        scratch_shapes=[
            pltpu.VMEM((C, 5184), BF16),
            pltpu.VMEM((C, 5184), BF16),
            pltpu.VMEM((5184, C), BF16),
            pltpu.VMEM((5184, C), BF16),
            pltpu.VMEM((2, 4, 2, C, W), BF16),
            pltpu.VMEM((2, 4, 2, C, W), BF16),
            pltpu.VMEM((2, 4, 2, C, W), BF16),
            pltpu.VMEM((2, 5184, 2 * W), BF16),
            pltpu.VMEM((2, 2, C, W), BF16),
            pltpu.VMEM((3 * C, 4 * W), BF16),
            pltpu.VMEM((3 * C, 2 * W), F32),
            pltpu.VMEM((2, C, W), BF16),
            pltpu.VMEM((2, 2, 2, 6, CHUNK, W), BF16),
            pltpu.VMEM((2, 3, 2, 6, 32, W), BF16),
            pltpu.VMEM((2, 3, 6, 64, W), BF16),
            pltpu.VMEM((2, 2, 6, 32, W), BF16),
            pltpu.VMEM((2, 6, 64, W), BF16),
            pltpu.VMEM((2, 3, 6, 16, W), BF16),
            pltpu.VMEM((2, 3, 6, 16, W), BF16),
            pltpu.VMEM((2, 2, 6, 16, W), BF16),
            pltpu.VMEM((2, 7, 2, 16, W), BF16),
            pltpu.VMEM((2, 3, 2, 2, 48, W), BF16),
            pltpu.VMEM((2, 3, 2, 2, 48, W), BF16),
            pltpu.VMEM((2, 4, 2, 2, 48, W), BF16),
            pltpu.VMEM((2, 2, 2, 48, W), BF16),
            pltpu.VMEM((2, 15, 16, W), BF16),
            pltpu.VMEM((2, 8, 3, 16, W), BF16),
            dma((4,)),
            dma((3, 7, 2)),
            dma((3, 2, 4, 2)),
            dma((2,)),
            dma((2, 2, 3)),
            dma((2, 2, 3)),
            dma((2, 2, 3)),
            dma((2, 2, 3)),
            dma((2, 7)),
            dma((2, 7)),
            dma((2, 3)),
            dma((2, 3)),
            dma((2, 4)),
            dma((2, 4)),
            dma((2, 15)),
            dma((2, 15)),
            dma((2, 7)),
            dma((2, 7)),
        ],
        compiler_params=pltpu.CompilerParams(
            collective_id=0, has_side_effects=True, vmem_limit_bytes=56 * 2**20
        ),
        cost_estimate=pl.CostEstimate(flops=2600000000, bytes_accessed=6000000, transcendentals=500000),
    )(video_in.reshape(2, C, W), jnp.swapaxes(kernels, 1, 2), cotangent.reshape(2, C, W))
    in_grad, k_grad = pl.pallas_call(
        finish,
        out_shape=(
            jax.ShapeDtypeStruct((2, 1, C, W), BF16),
            jax.ShapeDtypeStruct((162, 2, C), F32),
        ),
        in_specs=[vmem_spec, vmem_spec],
        out_specs=(vmem_spec, vmem_spec),
    )(in_grad, k_grad)
    return in_grad, jnp.swapaxes(k_grad, 0, 1)


def solution(mesh):
    return jax.shard_map(
        on_device,
        mesh=mesh,
        in_specs=(P("tm", "rows", None, None), P(), P("tm", "rows", None, None)),
        out_specs=(P("tm", "rows", None, None), P(None, "rows", None)),
        check_vma=False,
    )
```
